128 devices in a mesh: sec: 8 (over z, core), dom: 16 (over y, x).
Axes of the slice: x: 4, y: 4, z: 4, core: 2. Of those that a mesh axis runs over, the one named last changes fastest.
Arguments:
- fluid_state: bfloat16 [5, 125, 262144], P(None, None, ('sec', 'dom')), may hold values from -6 to 6
- jac_inv: float32 [262144], P(('sec', 'dom')), may hold values from 0.5 to 2
- flux_mats: float32 [3, 5, 5], replicated, may hold values from -2 to 2
- neighbours: int32 [6, 262144], P(None, ('sec', 'dom')), may hold values from 0 to 2559
- surf_elem: int32 [65536], P(('sec', 'dom')), may hold values from 0 to 2047
- surf_node: int32 [65536], P(('sec', 'dom')), may hold values from 0 to 124
- normals: float32 [3, 65536], P(None, ('sec', 'dom')), may hold values from -6 to 6
- rbf_weights: float32 [16, 65536], P(None, ('sec', 'dom')), may hold values from 0 to 0.25
- owners: int32 [65536, 1], P(('sec', 'dom')), may hold values from 0 to 15; in each aligned block of 512 rows (0 to 511, 512 to 1023, ...) at most 128 rows name the same one
- patches: int32 [65536], P(('sec', 'dom')), may hold values from 0 to 255
- patch_nodes: int32 [16, 4096], P(None, 'dom'), may hold values from 0 to 1023
- shell_disp: float32 [3, 16384], P(None, 'dom'), may hold values from -6 to 6
- shell_vel: float32 [3, 16384], P(None, 'dom'), may hold values from -6 to 6
- mass_inv: float32 [16384], P('dom'), may hold values from 0.5 to 2
- shell_conn: int32 [4, 16384], P(None, 'dom'), may hold values from 0 to 1087
- elem_scale: float32 [16384], P('dom'), may hold values from 0.5 to 2
- elem_stiff: float32 [12, 12], replicated, may hold values from -1.75 to 1.75
Outputs:
- fluid_next: bfloat16 [5, 125, 262144], P(None, None, ('sec', 'dom'))
- shell_next: float32 [3, 16384], P(None, 'dom')
- face_shift: float32 [3, 65536], P(None, ('sec', 'dom'))
The draws below stay inside these ranges and needn't reach their ends.
Inputs may be any that keep to these rules, and one draw needn't show every extreme that they name: `owners`: in the rows of one device no shell partition is named more than 128 times, a bound that some block reaches.
All inputs are finite; a program needn't handle non-finite values.
Results may differ from the reference program's by a relative error of at most 0.0065.
Values may be sent and summed in bfloat16 or wider, within the bound.
A program may use at most 128 MiB of HBM per device.

```python
import math
import jax
import jax.numpy as jnp
import numpy as np
from jax import lax

VARS = 5
NP = 125
K = 16
STEPS = 2
E_DEV = 2048
F_DEV = 512
PARTITION_PATCH = 256
S_DEV = 1024
SE_DEV = 1024
HALO = 256
HS = 32
CAP = 128
E_TOT = 262144
F_TOT = 65536
S_TOT = 16384
SE_TOT = 16384
TOTAL_PATCHES = 4096
N_SEC = 8
N_DOM = 16


def touch_ends(drawn, own_key, smallest, high):
    longest = drawn.shape.index(max(drawn.shape))
    spots = []
    for shift in (0, 1):
        where = [jax.random.randint(jax.random.fold_in(own_key, axis), (), 0, length) for axis, length in enumerate(drawn.shape)]
        where[longest] = (where[longest] + shift) % drawn.shape[longest]
        spots.append(tuple(where))
    return drawn.at[spots[0]].set(smallest).at[spots[1]].set(high)


def levels(rng, extent, shards, least, high):
    level, own = 1.0, jax.random.fold_in(rng, 6)
    for dim, blocks in shards:
        heights = jnp.exp(jax.random.uniform(jax.random.fold_in(own, dim), (blocks,), jnp.float32, least / len(shards), high / len(shards)))
        level = level * jnp.repeat(heights, extent[dim] // blocks).reshape([-1 if axis == dim else 1 for axis in range(len(extent))])
    return level


def routed_block(key, own, number, rows, number_of, top, bound, slope):
    sequence = jax.random.permutation(key, number_of)
    heavy_load, common = portions_of(number_of, rows * top, bound, slope, True), portions_of(number_of, rows * top, bound, slope, False)
    places = jnp.arange(number_of)

    def named(sizes, turn):
        used = int((sizes > 0).sum())
        fixed = max(1, used // 4)
        moved = fixed + (places - fixed + turn * (used - fixed)) % max(1, number_of - fixed)
        return jnp.zeros((number_of,), jnp.int32).at[sequence[jnp.where(places < fixed, places, moved)]].set(jnp.asarray(sizes, jnp.int32))

    sizes = jnp.where(number % 4 == 0, named(heavy_load, number // 4), named(common, number - number // 4 - 1))
    mixed = jax.random.permutation(jax.random.fold_in(own, 3), number_of)
    giver, sink = mixed[0:number_of // 2 * 2:2], mixed[1:number_of // 2 * 2:2]
    slack = jnp.minimum(sizes[giver] - 1, bound - sizes[sink]) // 2
    slack = jnp.where((giver == sequence[0]) | (sink == sequence[0]) | (sizes[sink] == 0), 0, jnp.maximum(slack, 0))
    moved = jax.random.randint(jax.random.fold_in(own, 4), (number_of // 2,), 0, 1 << 20) % (slack + 1)
    sizes = sizes.at[giver].add(-moved).at[sink].add(moved)
    labels = jnp.searchsorted(jnp.cumsum(sizes), jnp.arange(rows * top), side="right").astype(jnp.int32)
    listing = labels.reshape(top, rows).T
    listing = listing[jax.random.permutation(jax.random.fold_in(own, 1), rows)]
    turn = jax.random.randint(jax.random.fold_in(own, 2), (rows, 1), 0, top)
    return jnp.take_along_axis(listing, (jnp.arange(top)[None, :] + turn) % top, axis=1)


def portions_of(count, total, most, skew, full):
    portions = [(1 << 20) // math.isqrt(standing ** skew) + 1 for standing in range(1, count + 1)]
    largest = most if full else min(most, max(-(-total // count), total * portions[0] // sum(portions)))
    least = 1 if total - largest >= count - 1 else 0
    given, surplus = [largest] + [least] * (count - 1), total - largest - least * (count - 1)
    while surplus > 0:
        candidates = [i for i in range(1, count) if given[i] < largest] or [i for i in range(1, count) if given[i] < most]
        mass, budget = sum([portions[i] for i in candidates]), surplus
        for i in candidates:
            addition = min(most - given[i], max(1, budget * portions[i] // mass), surplus)
            given[i] = given[i] + addition
            surplus = surplus - addition
    return np.array(given)


def bell_draw(rng, dims, scale, bound, pieces=(), kind=jnp.bfloat16):
    gain = levels(rng, dims, pieces, -0.22, 0.18) if pieces else 1.0
    drawn = jax.random.normal(rng, dims, jnp.float32) * scale * gain
    return jnp.minimum(jnp.maximum(drawn, -bound), bound).astype(kind)


def setup_inputs(seed: int = 0) -> dict:
    seeds = jax.random.split(jax.random.key(seed), 18)
    fluid_state = bell_draw(seeds[0], (VARS, NP, E_TOT), 1.0, 6.0, ((2, 128),))
    jac_inv = jnp.clip(jnp.exp(math.log(2.0) - 1.3862944 * jax.random.uniform(seeds[1], (E_TOT,), jnp.float32) ** levels(seeds[1], (E_TOT,), ((0, 128),), -0.2, 0.2)), 0.5, 2.0)
    flux_mats = bell_draw(seeds[2], (3, VARS, VARS), 0.4, 2.0, (), jnp.float32)
    neighbours = touch_ends(jax.random.randint(seeds[3], (6, E_TOT), 0, E_DEV + 2 * HALO), jax.random.fold_in(seeds[3], 1), 0, (E_DEV + 2 * HALO) - 1).astype(jnp.int32)
    surf_elem = touch_ends(jax.random.randint(seeds[4], (F_TOT,), 0, E_DEV), jax.random.fold_in(seeds[4], 1), 0, E_DEV - 1).astype(jnp.int32)
    surf_node = touch_ends(jax.random.randint(seeds[5], (F_TOT,), 0, NP), jax.random.fold_in(seeds[5], 1), 0, NP - 1).astype(jnp.int32)
    normals = bell_draw(seeds[6], (3, F_TOT), 1.0, 6.0, ((1, 128),), jnp.float32)
    rbf_weights = jnp.clip(0.25 * jax.random.uniform(seeds[7], (K, F_TOT), jnp.float32) ** levels(seeds[7], (K, F_TOT), ((1, 128),), -0.2, 0.2), 0.0, 0.25)
    owners_keys = jax.random.split(jax.random.fold_in(seeds[8], 1), F_TOT // F_DEV)
    owners_turns = jax.random.permutation(jax.random.fold_in(seeds[8], 3), F_TOT // F_DEV)
    owners = jax.vmap(lambda own, number: routed_block(jax.random.fold_in(seeds[8], 2), own, number, F_DEV, N_DOM, 1, CAP, 2))(owners_keys, owners_turns).reshape((F_TOT, 1))
    patches = touch_ends(jax.random.randint(seeds[9], (F_TOT,), 0, PARTITION_PATCH), jax.random.fold_in(seeds[9], 1), 0, PARTITION_PATCH - 1).astype(jnp.int32)
    patch_nodes = touch_ends(jax.random.randint(seeds[10], (K, TOTAL_PATCHES), 0, S_DEV), jax.random.fold_in(seeds[10], 1), 0, S_DEV - 1).astype(jnp.int32)
    shell_disp = bell_draw(seeds[11], (3, S_TOT), 1.0, 6.0, ((1, 16),), jnp.float32)
    shell_vel = bell_draw(seeds[12], (3, S_TOT), 1.0, 6.0, ((1, 16),), jnp.float32)
    mass_inv = jnp.clip(jnp.exp(math.log(2.0) - 1.3862944 * jax.random.uniform(seeds[13], (S_TOT,), jnp.float32) ** levels(seeds[13], (S_TOT,), ((0, 16),), -0.2, 0.2)), 0.5, 2.0)
    shell_conn = touch_ends(jax.random.randint(seeds[14], (4, SE_TOT), 0, S_DEV + 2 * HS), jax.random.fold_in(seeds[14], 1), 0, (S_DEV + 2 * HS) - 1).astype(jnp.int32)
    elem_scale = jnp.clip(jnp.exp(math.log(2.0) - 1.3862944 * jax.random.uniform(seeds[15], (SE_TOT,), jnp.float32) ** levels(seeds[15], (SE_TOT,), ((0, 16),), -0.2, 0.2)), 0.5, 2.0)
    elem_stiff = bell_draw(seeds[16], (12, 12), 12 ** -0.5, 1.75, (), jnp.float32)
    return dict(fluid_state=fluid_state, jac_inv=jac_inv, flux_mats=flux_mats, neighbours=neighbours, surf_elem=surf_elem, surf_node=surf_node, normals=normals, rbf_weights=rbf_weights, owners=owners, patches=patches, patch_nodes=patch_nodes, shell_disp=shell_disp, shell_vel=shell_vel, mass_inv=mass_inv, shell_conn=shell_conn, elem_scale=elem_scale, elem_stiff=elem_stiff)


LIFT = 10.0
FLOW_STEP = 0.02
SHELL_STEP = 0.3

def lgl_derivative():
    points = np.array([-1.0, -np.sqrt(3.0 / 7.0), 0.0, np.sqrt(3.0 / 7.0), 1.0])
    barycentric = np.array([1.0 / np.prod([points[col] - points[other] for other in range(5) if other != col]) for col in range(5)])
    derivative = np.zeros((5, 5))
    for row in range(5):
        for col in range(5):
            if row != col:
                derivative[row, col] = barycentric[col] / barycentric[row] / (points[row] - points[col])
        derivative[row, row] = -np.sum(derivative[row])
    return derivative.astype(np.float32)

def face_traces(cube):
    width = cube.shape[0]
    count = cube.shape[-1]
    faces = [cube[:, 0], cube[:, 4], cube[:, :, 0], cube[:, :, 4], cube[:, :, :, 0], cube[:, :, :, 4]]
    return jnp.stack([face.reshape(width, 25, count) for face in faces])

def lift_faces(term_list, count):
    width = term_list.shape[1]
    shaped = term_list.reshape(6, width, 5, 5, count)
    lifted = jnp.zeros((width, 5, 5, 5, count), jnp.float32)
    lifted = lifted.at[:, 0].add(shaped[0])
    lifted = lifted.at[:, 4].add(shaped[1])
    lifted = lifted.at[:, :, 0].add(shaped[2])
    lifted = lifted.at[:, :, 4].add(shaped[3])
    lifted = lifted.at[:, :, :, 0].add(shaped[4])
    lifted = lifted.at[:, :, :, 4].add(shaped[5])
    return lifted

def fluid_tendency(cube, own_faces, extended_faces, neighbours, jac_inv, flux_mats):
    upper_limit = lax.Precision.HIGHEST
    derivative = jnp.asarray(lgl_derivative())
    count = cube.shape[-1]
    width = cube.shape[0]
    wide = cube.astype(jnp.float32)
    penalty = jnp.max(lax.optimization_barrier(jnp.sum(jnp.abs(flux_mats), axis=2)))
    flux_x = jnp.einsum('vw,wijke->vijke', flux_mats[0], wide, precision=upper_limit)
    flux_y = jnp.einsum('vw,wijke->vijke', flux_mats[1], wide, precision=upper_limit)
    flux_z = jnp.einsum('vw,wijke->vijke', flux_mats[2], wide, precision=upper_limit)
    divergence = jnp.einsum('ai,vijke->vajke', derivative, flux_x, precision=upper_limit)
    divergence = divergence + jnp.einsum('bj,vijke->vibke', derivative, flux_y, precision=upper_limit)
    divergence = divergence + jnp.einsum('ck,vijke->vijce', derivative, flux_z, precision=upper_limit)
    term_list = []
    for face in range(6):
        other = jnp.take(extended_faces[face ^ 1], neighbours[face], axis=2).astype(jnp.float32)
        interface_jump = own_faces[face].astype(jnp.float32) - other
        sign = 1.0 if face % 2 else -1.0
        coupling_pass = 0.5 * (sign * flux_mats[face // 2] - penalty * jnp.eye(width, dtype=jnp.float32))
        term_list.append(jnp.einsum('tk,kri->tri', coupling_pass, interface_jump, precision=upper_limit))
    lifted = lift_faces(jnp.stack(term_list), count)
    return jac_inv * (LIFT * lifted - divergence)

def reference(fluid_state, jac_inv, flux_mats, neighbours, surf_elem, surf_node, normals, rbf_weights, owners, patches, patch_nodes, shell_disp, shell_vel, mass_inv, shell_conn, elem_scale, elem_stiff):
    devices = N_SEC * N_DOM

    def fluid_device(index):
        start = index * E_DEV
        local = lax.dynamic_slice_in_dim(fluid_state, start, E_DEV, 2)
        before = lax.dynamic_slice_in_dim(fluid_state, jnp.maximum(start - HALO, 0).astype(jnp.int32), HALO, 2)
        after = lax.dynamic_slice_in_dim(fluid_state, jnp.minimum(start + E_DEV, E_TOT - HALO).astype(jnp.int32), HALO, 2)
        before = jnp.where(index > 0, before, jnp.zeros_like(before))
        after = jnp.where(index < devices - 1, after, jnp.zeros_like(after))
        extended = jnp.concatenate([before, local, after], axis=2)
        cube = local.reshape(VARS, 5, 5, 5, E_DEV)
        extended_faces = face_traces(extended.reshape(VARS, 5, 5, 5, E_DEV + 2 * HALO))
        own_faces = face_traces(cube)
        local_neighbours = lax.dynamic_slice_in_dim(neighbours, start, E_DEV, 1)
        local_jac = lax.dynamic_slice_in_dim(jac_inv, start, E_DEV, 0)
        tendency = fluid_tendency(cube, own_faces, extended_faces, local_neighbours, local_jac, flux_mats)
        new_state = (local.astype(jnp.float32) + FLOW_STEP * tendency.reshape(VARS, NP, E_DEV)).astype(jnp.bfloat16)
        row_start = index * F_DEV
        elems = lax.dynamic_slice_in_dim(surf_elem, row_start, F_DEV, 0)
        nodes = lax.dynamic_slice_in_dim(surf_node, row_start, F_DEV, 0)
        local_normals = lax.dynamic_slice_in_dim(normals, row_start, F_DEV, 1)
        pressure = new_state[4][nodes, elems].astype(jnp.float32)
        return (new_state, local_normals * pressure)
    states, tractions = lax.map(fluid_device, jnp.arange(devices, dtype=jnp.int32))
    fluid_next = jnp.moveaxis(states, 0, 2).reshape(VARS, NP, E_TOT)
    traction = jnp.moveaxis(tractions, 0, 1).reshape(3, F_TOT)
    owner_dom = owners[:, 0]
    node_list = owner_dom[None, :] * S_DEV + patch_nodes[:, owner_dom * PARTITION_PATCH + patches]
    contributions = traction[:, None, :] * rbf_weights[None]
    external = jnp.zeros((3, S_TOT), jnp.float32).at[:, node_list.reshape(-1)].add(contributions.reshape(3, -1))
    block = (jnp.arange(SE_TOT, dtype=jnp.int32) // SE_DEV)[None, :]
    global_nodes = block * S_DEV + shell_conn - HS
    gather_ok = ((global_nodes >= 0) & (global_nodes < S_TOT)).astype(jnp.float32)
    gather_index = jnp.clip(global_nodes, 0, S_TOT - 1)
    local_ok = ((shell_conn >= HS) & (shell_conn < HS + S_DEV)).astype(jnp.float32)
    displacement, velocity = (shell_disp, shell_vel)
    for substep in range(STEPS):
        picked = displacement[:, gather_index] * gather_ok
        elem_force = jnp.dot(elem_stiff, picked.reshape(12, SE_TOT), precision=lax.Precision.HIGHEST, preferred_element_type=jnp.float32) * elem_scale
        spread = (elem_force.reshape(3, 4, SE_TOT) * local_ok).reshape(3, -1)
        internal = jnp.zeros((3, S_TOT), jnp.float32).at[:, gather_index.reshape(-1)].add(spread)
        velocity = velocity + SHELL_STEP * mass_inv * (external - internal)
        displacement = displacement + SHELL_STEP * velocity
    face_shift = lax.optimization_barrier(jnp.sum(displacement[:, node_list] * rbf_weights[None], axis=1))
    return (fluid_next, displacement, face_shift)
```

```python
import jax
import jax.numpy as jnp
import numpy as np
from jax import lax
from jax.experimental import pallas as pl
from jax.experimental.pallas import tpu as pltpu
from jax.sharding import PartitionSpec as P

VARS, NP, K, STEPS = 5, 125, 16, 2
E, F, PATCHES, S, SE = 2048, 512, 256, 1024, 1024
HALO, HS, CAP = 256, 32, 128
N_SEC, N_DOM = 8, 16
LIFT, FLOW_STEP, SHELL_STEP = 10.0, 0.02, 0.3

TILE = 256
PART = 512
PARTS = (E + 2 * HALO) // PART
ROWS = VARS * 128
DEPTH = ROWS + 6 * 128
BF, F32, I32 = jnp.bfloat16, jnp.float32, jnp.int32
HIGHEST = lax.Precision.HIGHEST
MESH = pl.DeviceIdType.MESH


def lgl_derivative():
    points = np.array([-1.0, -np.sqrt(3.0 / 7.0), 0.0, np.sqrt(3.0 / 7.0), 1.0])
    barycentric = np.array(
        [
            1.0 / np.prod([points[col] - points[other] for other in range(5) if other != col])
            for col in range(5)
        ]
    )
    derivative = np.zeros((5, 5))
    for row in range(5):
        for col in range(5):
            if row != col:
                derivative[row, col] = (
                    barycentric[col] / barycentric[row] / (points[row] - points[col])
                )
        derivative[row, row] = -np.sum(derivative[row])
    return derivative.astype(np.float32)


def constants():
    nodes = np.arange(NP).reshape(5, 5, 5)
    faces = [nodes[0], nodes[4], nodes[:, 0], nodes[:, 4], nodes[:, :, 0], nodes[:, :, 4]]
    faces = [face.reshape(25) for face in faces]
    d, eye = lgl_derivative(), np.eye(5, dtype=np.float32)
    own = np.zeros((4, 128, 128), np.float32)
    own[0, :NP, :NP] = -np.kron(np.kron(d, eye), eye)
    own[1, :NP, :NP] = -np.kron(np.kron(eye, d), eye)
    own[2, :NP, :NP] = -np.kron(np.kron(eye, eye), d)
    for face in range(6):
        sign = 1.0 if face % 2 else -1.0
        for node in faces[face]:
            own[face // 2, node, node] += sign * 0.5 * LIFT
            own[3, node, node] -= 0.5 * LIFT
    select = np.zeros((VARS, 6 * 32, 128), np.float32)
    place = np.zeros((6, 128, 128), np.float32)
    for face in range(6):
        for n in range(25):
            for w in range(VARS):
                select[w, face * 32 + w + n, faces[face ^ 1][n]] = 1.0
                place[face, faces[face][n], 25 * w + n] = -0.5 * LIFT
    return own, select.astype(jnp.bfloat16), place.astype(jnp.bfloat16)


def dot(a, b):
    return jnp.dot(a, b, preferred_element_type=F32)


def dot_t(a, b):
    return lax.dot_general(a, b, (((1,), (1,)), ((), ())), preferred_element_type=F32)


def halves(x):
    high = x.astype(BF)
    low = (x - high.astype(F32)).astype(BF)
    return jnp.concatenate([high, low], axis=0)


def joined(y):
    rows = y.shape[0] // 2
    return y[:rows] + y[rows:]


def iota(shape, dim):
    return lax.broadcasted_iota(I32, shape, dim)


def one_hot(ids, rows):
    return (iota((rows, ids.shape[1]), 0) == ids).astype(F32)


def kernel(
    u_ref, jac_ref, flux_ref, nb_ref, selem_ref, snode_ref, normal_ref, weight_ref, owner_ref,
    patch_ref, pnode_ref, disp_ref, vel_ref, minv_ref, conn_ref, scale_ref, stiff_ref,
    own_ref, select_ref, place_ref,
    fluid_ref, shell_ref, shift_ref,
    x_ref, src_ref, ab_ref, hlo_ref, hhi_ref, o4_ref,
    ohp_ref, ohn_ref, maskn_ref, ohc_ref, maskc_ref, mask8_ref, ohs_ref,
    wsend_ref, wrecv_ref, wall_ref, tsend_ref, trecv_ref, rsend_ref, rrecv_ref,
    ebuf_ref, erecv_ref, edge_ref, rim_ref, d_ref, v_ref, m_ref,
    flow_s, flow_r, w_s, w_r, t_s, t_r, r_s, r_r, e_s, e_r, rim_s, rim_r,
):
    sec, dom = lax.axis_index("sec"), lax.axis_index("dom")
    line = sec * N_DOM + dom
    devices = N_SEC * N_DOM
    nxt, prv = lax.rem(line + 1, devices), lax.rem(line + devices - 1, devices)
    right = (nxt // N_DOM, lax.rem(nxt, N_DOM))
    left = (prv // N_DOM, lax.rem(prv, N_DOM))

    def dom_peer(d):
        return (sec, lax.rem(dom + d, N_DOM))

    def sec_peer(d):
        return (lax.rem(sec + d, N_SEC), dom)

    def copy(src, dst, send, recv, device):
        return pltpu.make_async_remote_copy(
            src_ref=src, dst_ref=dst, send_sem=send, recv_sem=recv, device_id=device, device_id_type=MESH
        )

    barrier = pltpu.get_barrier_semaphore()
    greeted = [dom_peer(d) for d in range(1, N_DOM)] + [sec_peer(d) for d in range(1, N_SEC)] + [right, left]
    for device in greeted:
        pl.semaphore_signal(barrier, inc=1, device_id=device, device_id_type=MESH)

    for v in range(VARS):
        x_ref[v * 128 + 112 : v * 128 + 128, :] = jnp.zeros((16, E), BF)
        x_ref[v * 128 : v * 128 + NP, :] = u_ref[v]

    for h in range(8):
        lanes = slice(h * 128, (h + 1) * 128)
        m_ref[h : h + 1, :] = minv_ref[:, lanes]
        for c in range(3):
            d_ref[c * 8 + h : c * 8 + h + 1, :] = disp_ref[c : c + 1, lanes]
            v_ref[c * 8 + h : c * 8 + h + 1, :] = vel_ref[c : c + 1, lanes]

    relative = (owner_ref[...] - dom + N_DOM) & (N_DOM - 1)
    owned = one_hot(relative, N_DOM)
    earlier = (iota((F, F), 0) < iota((F, F), 1)).astype(F32).astype(BF)
    rank = jnp.sum(owned * dot(owned.astype(BF), earlier), axis=0, keepdims=True).astype(I32)
    ohs_ref[...] = one_hot(rank, CAP).astype(BF)

    payload = jnp.concatenate([weight_ref[...], patch_ref[...].astype(F32), jnp.zeros((15, F), F32)], axis=0)
    payload = jnp.concatenate([payload * owned[d : d + 1] for d in range(N_DOM)], axis=0)
    placed = dot_t(payload.astype(BF), ohs_ref[...])
    wsend_ref[...] = placed.astype(BF).reshape(N_DOM, 32, CAP)

    def edges(step):
        for c in range(3):
            edge_ref[step, 0, c : c + 1, :] = d_ref[c * 8 : c * 8 + 1, :]
            edge_ref[step, 1, c : c + 1, :] = d_ref[c * 8 + 7 : c * 8 + 8, :]

    def rims(step):
        return [
            copy(edge_ref.at[step, 0], rim_ref.at[step, 0], rim_s.at[step, 0], rim_r.at[step, 0], dom_peer(N_DOM - 1)),
            copy(edge_ref.at[step, 1], rim_ref.at[step, 1], rim_s.at[step, 1], rim_r.at[step, 1], dom_peer(1)),
        ]

    edge_ref[...] = jnp.zeros(edge_ref.shape, F32)
    edges(0)

    pl.semaphore_wait(barrier, len(greeted))
    flow = [
        copy(x_ref.at[0:ROWS, E - HALO : E], hlo_ref, flow_s.at[0], flow_r.at[0], right),
        copy(x_ref.at[0:ROWS, 0:HALO], hhi_ref, flow_s.at[1], flow_r.at[1], left),
    ]
    for c in flow:
        c.start()
    early = [copy(wsend_ref.at[d], wrecv_ref.at[d], w_s.at[d], w_r.at[d], dom_peer(d)) for d in range(1, N_DOM)]
    for c in early:
        c.start()
    wrecv_ref[0] = wsend_ref[0]
    rim0 = rims(0)
    for c in rim0:
        c.start()

    penalty = None
    for d in range(3):
        for v in range(VARS):
            total = jnp.abs(flux_ref[d, v, 0])
            for w in range(1, VARS):
                total = total + jnp.abs(flux_ref[d, v, w])
            penalty = total if penalty is None else jnp.maximum(penalty, total)
    for v in range(VARS):
        for w in range(VARS):
            block = flux_ref[0, v, w] * own_ref[0] + flux_ref[1, v, w] * own_ref[1] + flux_ref[2, v, w] * own_ref[2]
            if v == w:
                block = block + penalty * own_ref[3]
            ab_ref[v * 128 : v * 128 + 128, w * 128 : w * 128 + 128] = block.astype(BF)
    column = iota((1, 128), 1)
    for face in range(6):
        sign = 1.0 if face % 2 else -1.0
        where = place_ref[face].astype(F32)
        for v in range(VARS):
            factor = jnp.zeros((1, 128), F32)
            for w in range(VARS):
                value = sign * flux_ref[face // 2, v, w]
                if v == w:
                    value = value - penalty
                factor = jnp.where((column >= 25 * w) & (column < 25 * w + 25), value, factor)
            ab_ref[v * 128 : v * 128 + 128, ROWS + face * 128 : ROWS + face * 128 + 128] = (where * factor).astype(BF)

    def extract(values, part, lanes):
        e = [dot(select_ref[w], values(w)) for w in range(VARS)]
        for face in range(6):
            g = [x[face * 32 : face * 32 + 32] for x in e]
            pieces = [g[0][0:24]]
            for w in range(1, VARS):
                pieces += [g[w - 1][24:32] + g[w][0:8], g[w][8:24]]
            pieces += [g[VARS - 1][24:32]]
            src_ref[face, pl.ds(part * 128, 128), lanes] = jnp.concatenate(pieces, axis=0).astype(BF)

    for part in range(E // PART):
        for half in range(PART // TILE):
            cols = slice(part * PART + half * TILE, part * PART + (half + 1) * TILE)
            extract(lambda w: x_ref[w * 128 : w * 128 + 128, cols], part, slice(half * TILE, (half + 1) * TILE))

    for k in range(K):
        ids = pnode_ref[k : k + 1, :]
        lanes = slice(k * PATCHES, (k + 1) * PATCHES)
        ohn_ref[:, lanes] = one_hot(ids & 127, 128).astype(BF)
        maskn_ref[:, lanes] = one_hot(ids >> 7, 8)
    for q in range(4):
        ids = conn_ref[q : q + 1, :]
        ids = jnp.where(ids >= HS, ids - HS, ids + (S + 128 - HS))
        lanes = slice(q * SE, (q + 1) * SE)
        ohc_ref[:, lanes] = one_hot(ids & 127, 128).astype(BF)
        maskc_ref[:, lanes] = one_hot(ids >> 7, 8)
        mask8_ref[:, lanes] = ((ids >> 7) == 8).astype(F32)

    for c in flow:
        c.wait()
    keep_hi = jnp.where(line < devices - 1, 1.0, 0.0).astype(BF)
    keep_lo = jnp.where(line > 0, 1.0, 0.0).astype(BF)
    extract(lambda w: hhi_ref[w * 128 : w * 128 + 128, :] * keep_hi, PARTS - 1, slice(0, HALO))
    extract(lambda w: hlo_ref[w * 128 : w * 128 + 128, :] * keep_lo, PARTS - 1, slice(HALO, 2 * HALO))

    def gather(t, carry):
        cols = pl.ds(pl.multiple_of(t * TILE, TILE), TILE)
        for face in range(6):
            ids = nb_ref[face : face + 1, cols]
            ids = jnp.where(ids >= HALO, ids - HALO, ids + (E + HALO))
            picked = dot(src_ref[face], one_hot(ids & (PART - 1), PART).astype(BF))
            part = ids // PART
            other = picked[0:128]
            for p in range(1, PARTS):
                other = jnp.where(part == p, picked[p * 128 : p * 128 + 128], other)
            x_ref[ROWS + face * 128 : ROWS + face * 128 + 128, cols] = other.astype(BF)
        factor = FLOW_STEP * jac_ref[:, cols]
        v = VARS - 1
        moved = x_ref[v * 128 : v * 128 + 128, cols].astype(F32) + factor * dot(
            ab_ref[v * 128 : v * 128 + 128, :], x_ref[:, cols]
        )
        moved = moved.astype(BF)
        o4_ref[:, cols] = moved
        fluid_ref[v, :, cols] = moved[:NP]
        return carry

    lax.fori_loop(0, E // TILE, gather, 0)

    elems = selem_ref[...]
    picker = one_hot(elems & (TILE - 1), TILE).astype(BF)
    found = jnp.zeros((128, F), F32)
    for h in range(E // TILE):
        found = jnp.where((elems // TILE) == h, dot(o4_ref[:, h * TILE : (h + 1) * TILE], picker), found)
    pressure = jnp.sum(jnp.where(iota((128, F), 0) == snode_ref[...], found, 0.0), axis=0, keepdims=True)
    traction = jnp.concatenate([normal_ref[...] * pressure, jnp.zeros((5, F), F32)], axis=0)
    rows = jnp.concatenate([traction * owned[d : d + 1] for d in range(N_DOM)], axis=0)
    tsend_ref[...] = joined(dot_t(halves(rows), ohs_ref[...])).reshape(N_DOM, 8, CAP)
    loads = [copy(tsend_ref.at[d], trecv_ref.at[d], t_s.at[d], t_r.at[d], dom_peer(d)) for d in range(1, N_DOM)]
    for c in loads:
        c.start()
    trecv_ref[0] = tsend_ref[0]

    def advance(t, carry):
        cols = pl.ds(pl.multiple_of(t * TILE, TILE), TILE)
        factor = FLOW_STEP * jac_ref[:, cols]
        change = dot(ab_ref[0 : 4 * 128, :], x_ref[:, cols])
        for v in range(VARS - 1):
            moved = x_ref[v * 128 : v * 128 + 128, cols].astype(F32) + factor * change[v * 128 : v * 128 + 128]
            fluid_ref[v, :, cols] = moved.astype(BF)[:NP]
        return carry

    lax.fori_loop(0, E // TILE, advance, 0)

    for c in early:
        c.wait()
    for d in range(N_DOM):
        block = wrecv_ref[d].astype(F32)
        wall_ref[:, d * CAP : (d + 1) * CAP] = block[0:K]
        ohp_ref[:, d * CAP : (d + 1) * CAP] = one_hot(block[K : K + 1].astype(I32), PATCHES).astype(BF)

    def internal(step):
        lane = iota((8, 128), 1)
        from_right = rim_ref[step, 0] * jnp.where(dom < N_DOM - 1, 1.0, 0.0)
        from_left = rim_ref[step, 1] * jnp.where(dom > 0, 1.0, 0.0)
        rim = jnp.where(lane < 64, from_right, from_left)
        read = joined(dot(halves(jnp.concatenate([d_ref[...], rim], axis=0)), ohc_ref[...]))
        picked = []
        for c in range(3):
            values = jnp.sum(read[c * 8 : c * 8 + 8] * maskc_ref[...], axis=0, keepdims=True)
            values = values + read[24 + c : 25 + c] * mask8_ref[...]
            picked += [values[:, q * SE : (q + 1) * SE] for q in range(4)]
        force = jnp.dot(
            stiff_ref[...], jnp.concatenate(picked, axis=0), precision=HIGHEST, preferred_element_type=F32
        )
        force = force * scale_ref[...]
        spread = []
        for c in range(3):
            line_c = jnp.concatenate([force[c * 4 + q : c * 4 + q + 1] for q in range(4)], axis=1)
            spread.append(line_c * maskc_ref[...])
        return joined(dot_t(halves(jnp.concatenate(spread, axis=0)), ohc_ref[...]))

    for c in rim0:
        c.wait()
    inner = internal(0)

    for c in loads:
        c.wait()
    load = []
    for c in range(3):
        line_c = jnp.concatenate([trecv_ref[d, c : c + 1, :] for d in range(N_DOM)], axis=1)
        load.append(wall_ref[...] * line_c)
    by_patch = joined(dot_t(halves(jnp.concatenate(load, axis=0)), ohp_ref[...]))
    spread = []
    for c in range(3):
        line_c = jnp.concatenate([by_patch[c * K + k : c * K + k + 1] for k in range(K)], axis=1)
        spread.append(line_c * maskn_ref[...])
    partial = joined(dot_t(halves(jnp.concatenate(spread, axis=0)), ohn_ref[...]))
    ebuf_ref[...] = partial
    sums = [copy(ebuf_ref, erecv_ref.at[d], e_s.at[d], e_r.at[d], sec_peer(d)) for d in range(1, N_SEC)]
    for c in sums:
        c.start()
    erecv_ref[0] = partial
    for c in sums:
        c.wait()
    external = erecv_ref[lax.rem(sec, N_SEC)]
    for s in range(1, N_SEC):
        external = external + erecv_ref[lax.rem(sec - s + N_SEC, N_SEC)]

    mass = jnp.concatenate([m_ref[...]] * 3, axis=0)
    for step in range(STEPS):
        if step > 0:
            edges(step)
            around = rims(step)
            for c in around:
                c.start()
            for c in around:
                c.wait()
            inner = internal(step)
        velocity = v_ref[...] + SHELL_STEP * mass * (external - inner)
        v_ref[...] = velocity
        d_ref[...] = d_ref[...] + SHELL_STEP * velocity

    read = joined(dot(halves(d_ref[...]), ohn_ref[...]))
    nodes = []
    for c in range(3):
        values = jnp.sum(read[c * 8 : c * 8 + 8] * maskn_ref[...], axis=0, keepdims=True)
        nodes += [values[:, k * PATCHES : (k + 1) * PATCHES] for k in range(K)]
    by_row = joined(dot(halves(jnp.concatenate(nodes, axis=0)), ohp_ref[...]))
    rsend_ref[...] = jnp.zeros(rsend_ref.shape, F32)
    for c in range(3):
        total = jnp.sum(by_row[c * K : (c + 1) * K] * wall_ref[...], axis=0, keepdims=True)
        for d in range(N_DOM):
            rsend_ref[d, c : c + 1, :] = total[:, d * CAP : (d + 1) * CAP]
    returns = [
        copy(rsend_ref.at[d], rrecv_ref.at[d], r_s.at[d], r_r.at[d], dom_peer(N_DOM - d)) for d in range(1, N_DOM)
    ]
    for c in returns:
        c.start()
    rrecv_ref[0] = rsend_ref[0]
    for h in range(8):
        for c in range(3):
            shell_ref[c : c + 1, h * 128 : (h + 1) * 128] = d_ref[c * 8 + h : c * 8 + h + 1, :]
    for c in returns:
        c.wait()
    back = joined(dot(halves(rrecv_ref[...].reshape(N_DOM * 8, CAP)), ohs_ref[...]))
    shift = back[0:8] * owned[0:1]
    for d in range(1, N_DOM):
        shift = shift + back[d * 8 : d * 8 + 8] * owned[d : d + 1]
    shift_ref[...] = shift[0:3]


def on_device(
    fluid_state, jac_inv, flux_mats, neighbours, surf_elem, surf_node, normals, rbf_weights, owners,
    patches, patch_nodes, shell_disp, shell_vel, mass_inv, shell_conn, elem_scale, elem_stiff,
):
    own, select, place = constants()
    vmem, smem = pl.BlockSpec(memory_space=pltpu.VMEM), pl.BlockSpec(memory_space=pltpu.SMEM)
    dma = pltpu.SemaphoreType.DMA
    return pl.pallas_call(
        kernel,
        out_shape=(
            jax.ShapeDtypeStruct((VARS, NP, E), BF),
            jax.ShapeDtypeStruct((3, S), F32),
            jax.ShapeDtypeStruct((3, F), F32),
        ),
        in_specs=[vmem, vmem, smem] + [vmem] * 17,
        out_specs=(vmem, vmem, vmem),
        scratch_shapes=[
            pltpu.VMEM((DEPTH, E), BF),
            pltpu.VMEM((6, PARTS * 128, PART), BF),
            pltpu.VMEM((ROWS, DEPTH), BF),
            pltpu.VMEM((ROWS, HALO), BF),
            pltpu.VMEM((ROWS, HALO), BF),
            pltpu.VMEM((128, E), BF),
            pltpu.VMEM((PATCHES, N_DOM * CAP), BF),
            pltpu.VMEM((128, K * PATCHES), BF),
            pltpu.VMEM((8, K * PATCHES), F32),
            pltpu.VMEM((128, 4 * SE), BF),
            pltpu.VMEM((8, 4 * SE), F32),
            pltpu.VMEM((1, 4 * SE), F32),
            pltpu.VMEM((CAP, F), BF),
            pltpu.VMEM((N_DOM, 32, CAP), BF),
            pltpu.VMEM((N_DOM, 32, CAP), BF),
            pltpu.VMEM((K, N_DOM * CAP), F32),
            pltpu.VMEM((N_DOM, 8, CAP), F32),
            pltpu.VMEM((N_DOM, 8, CAP), F32),
            pltpu.VMEM((N_DOM, 8, CAP), F32),
            pltpu.VMEM((N_DOM, 8, CAP), F32),
            pltpu.VMEM((24, 128), F32),
            pltpu.VMEM((N_SEC, 24, 128), F32),
            pltpu.VMEM((STEPS, 2, 8, 128), F32),
            pltpu.VMEM((STEPS, 2, 8, 128), F32),
            pltpu.VMEM((24, 128), F32),
            pltpu.VMEM((24, 128), F32),
            pltpu.VMEM((8, 128), F32),
            dma((2,)), dma((2,)),
            dma((N_DOM,)), dma((N_DOM,)),
            dma((N_DOM,)), dma((N_DOM,)),
            dma((N_DOM,)), dma((N_DOM,)),
            dma((N_SEC,)), dma((N_SEC,)),
            dma((STEPS, 2)), dma((STEPS, 2)),
        ],
        compiler_params=pltpu.CompilerParams(
            collective_id=0, has_side_effects=True, vmem_limit_bytes=56 * 1024 * 1024
        ),
    )(
        fluid_state, jac_inv.reshape(1, E), flux_mats, neighbours, surf_elem.reshape(1, F),
        surf_node.reshape(1, F), normals, rbf_weights, owners.reshape(1, F), patches.reshape(1, F),
        patch_nodes, shell_disp, shell_vel, mass_inv.reshape(1, S), shell_conn,
        elem_scale.reshape(1, SE), elem_stiff, jnp.asarray(own), jnp.asarray(select), jnp.asarray(place),
    )


def solution(mesh):
    flow, shell = ("sec", "dom"), "dom"
    return jax.shard_map(
        on_device,
        mesh=mesh,
        in_specs=(
            P(None, None, flow),
            P(flow),
            P(),
            P(None, flow),
            P(flow),
            P(flow),
            P(None, flow),
            P(None, flow),
            P(flow, None),
            P(flow),
            P(None, shell),
            P(None, shell),
            P(None, shell),
            P(shell),
            P(None, shell),
            P(shell),
            P(),
        ),
        out_specs=(P(None, None, flow), P(None, shell), P(None, flow)),
        check_vma=False,
    )
```

```python
import jax
import jax.numpy as jnp
import numpy as np
from jax import lax
from jax.experimental import pallas as pl
from jax.experimental.pallas import tpu as pltpu
from jax.sharding import PartitionSpec as P

VARS, NP, K, STEPS = 5, 125, 16, 2
E, F, PATCHES, S, SE = 2048, 512, 256, 1024, 1024
HALO, HS, CAP = 256, 32, 128
N_SEC, N_DOM = 8, 16
LIFT, FLOW_STEP, SHELL_STEP = 10.0, 0.02, 0.3

TILE = 256
PART = 512
PARTS = (E + 2 * HALO) // PART
ROWS = VARS * 128
DEPTH = ROWS + 6 * 128
BF, F32, I32 = jnp.bfloat16, jnp.float32, jnp.int32
HIGHEST = lax.Precision.HIGHEST
MESH = pl.DeviceIdType.MESH


def lgl_derivative():
    points = np.array([-1.0, -np.sqrt(3.0 / 7.0), 0.0, np.sqrt(3.0 / 7.0), 1.0])
    barycentric = np.array(
        [
            1.0 / np.prod([points[col] - points[other] for other in range(5) if other != col])
            for col in range(5)
        ]
    )
    derivative = np.zeros((5, 5))
    for row in range(5):
        for col in range(5):
            if row != col:
                derivative[row, col] = (
                    barycentric[col] / barycentric[row] / (points[row] - points[col])
                )
        derivative[row, row] = -np.sum(derivative[row])
    return derivative.astype(np.float32)


def constants():
    nodes = np.arange(NP).reshape(5, 5, 5)
    faces = [nodes[0], nodes[4], nodes[:, 0], nodes[:, 4], nodes[:, :, 0], nodes[:, :, 4]]
    faces = [face.reshape(25) for face in faces]
    d, eye = lgl_derivative(), np.eye(5, dtype=np.float32)
    own = np.zeros((4, 128, 128), np.float32)
    own[0, :NP, :NP] = -np.kron(np.kron(d, eye), eye)
    own[1, :NP, :NP] = -np.kron(np.kron(eye, d), eye)
    own[2, :NP, :NP] = -np.kron(np.kron(eye, eye), d)
    for face in range(6):
        sign = 1.0 if face % 2 else -1.0
        for node in faces[face]:
            own[face // 2, node, node] += sign * 0.5 * LIFT
            own[3, node, node] -= 0.5 * LIFT
    select = np.zeros((VARS, 6 * 32, 128), np.float32)
    place = np.zeros((6, 128, 128), np.float32)
    for face in range(6):
        for n in range(25):
            for w in range(VARS):
                select[w, face * 32 + w + n, faces[face ^ 1][n]] = 1.0
                place[face, faces[face][n], 25 * w + n] = -0.5 * LIFT
    return own, select.astype(jnp.bfloat16), place.astype(jnp.bfloat16)


def dot(a, b):
    return jnp.dot(a, b, preferred_element_type=F32)


def dot_t(a, b):
    return lax.dot_general(a, b, (((1,), (1,)), ((), ())), preferred_element_type=F32)


def halves(x):
    high = x.astype(BF)
    low = (x - high.astype(F32)).astype(BF)
    return jnp.concatenate([high, low], axis=0)


def joined(y):
    rows = y.shape[0] // 2
    return y[:rows] + y[rows:]


def iota(shape, dim):
    return lax.broadcasted_iota(I32, shape, dim)


def one_hot(ids, rows):
    return (iota((rows, ids.shape[1]), 0) == ids).astype(F32)


def kernel(
    state_ref, jac_ref, flux_ref, nb_ref, selem_ref, snode_ref, normal_ref, weight_ref, owner_ref,
    patch_ref, pnode_ref, disp_ref, vel_ref, minv_ref, conn_ref, scale_ref, stiff_ref,
    own_hbm, select_hbm, place_hbm,
    fluid_ref, shell_ref, shift_ref,
    u_ref, own_ref, select_ref, place_ref, x_ref, src_ref, ab_ref, hlo_ref, hhi_ref,
    surf_ref, ohp_ref, ohn_ref, maskn_ref, ohc_ref, maskc_ref, mask8_ref, ohs_ref,
    wsend_ref, wrecv_ref, wall_ref, tsend_ref, trecv_ref, rsend_ref, rrecv_ref,
    ebuf_ref, erecv_ref, edge_ref, rim_ref, d_ref, v_ref, m_ref,
    local_s, flow_s, flow_r, w_s, w_r, t_s, t_r, r_s, r_r, e_s, e_r, rim_s, rim_r,
):
    sec, dom = lax.axis_index("sec"), lax.axis_index("dom")
    line = sec * N_DOM + dom
    devices = N_SEC * N_DOM
    nxt, prv = lax.rem(line + 1, devices), lax.rem(line + devices - 1, devices)
    right = (nxt // N_DOM, lax.rem(nxt, N_DOM))
    left = (prv // N_DOM, lax.rem(prv, N_DOM))

    def dom_peer(d):
        return (sec, lax.rem(dom + d, N_DOM))

    def sec_peer(d):
        return (lax.rem(sec + d, N_SEC), dom)

    def copy(src, dst, send, recv, device):
        return pltpu.make_async_remote_copy(
            src_ref=src, dst_ref=dst, send_sem=send, recv_sem=recv, device_id=device, device_id_type=MESH
        )

    barrier = pltpu.get_barrier_semaphore()
    greeted = [dom_peer(d) for d in range(1, N_DOM)] + [sec_peer(d) for d in range(1, N_SEC)] + [right, left]
    for device in greeted:
        pl.semaphore_signal(barrier, inc=1, device_id=device, device_id_type=MESH)

    fetch = [
        pltpu.make_async_copy(src, dst, local_s.at[i])
        for i, (src, dst) in enumerate(
            ((state_ref, u_ref), (own_hbm, own_ref), (select_hbm, select_ref), (place_hbm, place_ref))
        )
    ]
    for c in fetch:
        c.start()

    for h in range(8):
        lanes = slice(h * 128, (h + 1) * 128)
        m_ref[h : h + 1, :] = minv_ref[:, lanes]
        for c in range(3):
            d_ref[c * 8 + h : c * 8 + h + 1, :] = disp_ref[c : c + 1, lanes]
            v_ref[c * 8 + h : c * 8 + h + 1, :] = vel_ref[c : c + 1, lanes]

    def edges(step):
        for c in range(3):
            edge_ref[step, 0, c : c + 1, :] = d_ref[c * 8 : c * 8 + 1, :]
            edge_ref[step, 1, c : c + 1, :] = d_ref[c * 8 + 7 : c * 8 + 8, :]

    def rims(step):
        return [
            copy(edge_ref.at[step, 0], rim_ref.at[step, 0], rim_s.at[step, 0], rim_r.at[step, 0], dom_peer(N_DOM - 1)),
            copy(edge_ref.at[step, 1], rim_ref.at[step, 1], rim_s.at[step, 1], rim_r.at[step, 1], dom_peer(1)),
        ]

    edge_ref[...] = jnp.zeros(edge_ref.shape, F32)
    edges(0)

    fetch[0].wait()
    for v in range(VARS):
        x_ref[v * 128 + 112 : v * 128 + 128, :] = jnp.zeros((16, E), BF)
        x_ref[v * 128 : v * 128 + NP, :] = u_ref[v]

    pl.semaphore_wait(barrier, len(greeted))
    rim0 = rims(0)
    for c in rim0:
        c.start()
    flow = [
        copy(x_ref.at[0:ROWS, E - HALO : E], hlo_ref, flow_s.at[0], flow_r.at[0], right),
        copy(x_ref.at[0:ROWS, 0:HALO], hhi_ref, flow_s.at[1], flow_r.at[1], left),
    ]
    for c in flow:
        c.start()

    for c in fetch[1:]:
        c.wait()
    penalty = None
    for v in range(VARS):
        total = jnp.max(jnp.sum(jnp.abs(flux_ref[v]), axis=1, keepdims=True), axis=0, keepdims=True)
        penalty = total if penalty is None else jnp.maximum(penalty, total)

    def flux(d, v, w):
        return flux_ref[v, d : d + 1, w : w + 1]

    for v in range(VARS):
        for w in range(VARS):
            block = flux(0, v, w) * own_ref[0] + flux(1, v, w) * own_ref[1] + flux(2, v, w) * own_ref[2]
            if v == w:
                block = block + penalty * own_ref[3]
            ab_ref[v * 128 : v * 128 + 128, w * 128 : w * 128 + 128] = block.astype(BF)
    column = iota((1, 128), 1)
    for face in range(6):
        sign = 1.0 if face % 2 else -1.0
        where = place_ref[face].astype(F32)
        for v in range(VARS):
            factor = jnp.zeros((1, 128), F32)
            for w in range(VARS):
                value = sign * flux(face // 2, v, w)
                if v == w:
                    value = value - penalty
                factor = jnp.where((column >= 25 * w) & (column < 25 * w + 25), value, factor)
            ab_ref[v * 128 : v * 128 + 128, ROWS + face * 128 : ROWS + face * 128 + 128] = (where * factor).astype(BF)

    def extract(values, part, lanes):
        e = [dot(select_ref[w], values(w)) for w in range(VARS)]
        for face in range(6):
            g = [x[face * 32 : face * 32 + 32] for x in e]
            pieces = [g[0][0:24]]
            for w in range(1, VARS):
                pieces += [g[w - 1][24:32] + g[w][0:8], g[w][8:24]]
            pieces += [g[VARS - 1][24:32]]
            src_ref[face, pl.ds(part * 128, 128), lanes] = jnp.concatenate(pieces, axis=0).astype(BF)

    for part in range(E // PART):
        for half in range(PART // TILE):
            cols = slice(part * PART + half * TILE, part * PART + (half + 1) * TILE)
            extract(lambda w: x_ref[w * 128 : w * 128 + 128, cols], part, slice(half * TILE, (half + 1) * TILE))

    relative = (owner_ref[...] - dom + N_DOM) & (N_DOM - 1)
    owned = one_hot(relative, N_DOM)
    earlier = (iota((F, F), 0) < iota((F, F), 1)).astype(F32).astype(BF)
    rank = jnp.sum(owned * dot(owned.astype(BF), earlier), axis=0, keepdims=True).astype(I32)
    ohs_ref[...] = one_hot(rank, CAP).astype(BF)

    payload = jnp.concatenate([weight_ref[...], patch_ref[...].astype(F32), jnp.zeros((15, F), F32)], axis=0)
    payload = jnp.concatenate([payload * owned[d : d + 1] for d in range(N_DOM)], axis=0)
    placed = dot_t(payload.astype(BF), ohs_ref[...])
    wsend_ref[...] = placed.astype(BF).reshape(N_DOM, 32, CAP)

    last = slice((VARS - 1) * 128, VARS * 128)
    elems = selem_ref[...]
    picker = one_hot(elems & (TILE - 1), TILE).astype(BF)
    base, near = jnp.zeros((128, F), F32), jnp.zeros((16, F), F32)
    for h in range(E // TILE):
        cols = slice(h * TILE, (h + 1) * TILE)
        factor = FLOW_STEP * jac_ref[:, cols]
        moved = x_ref[last, cols].astype(F32) + factor * dot(ab_ref[last, 0:ROWS], x_ref[0:ROWS, cols])
        ids = nb_ref[:, cols]
        rows = jnp.concatenate(
            [halves(factor), (ids & 255).astype(F32).astype(BF), (ids >> 8).astype(F32).astype(BF)], axis=0
        )
        rows = jnp.concatenate([halves(moved), rows, jnp.zeros((2, TILE), BF)], axis=0)
        found = dot(rows, picker)
        mine = (elems // TILE) == h
        base = jnp.where(mine, joined(found[0:256]), base)
        near = jnp.where(mine, found[256:272], near)
    surf_factor = near[0:1] + near[1:2]
    surf_near = near[2:8].astype(I32) + 256 * near[8:14].astype(I32)

    for k in range(K):
        ids = pnode_ref[k : k + 1, :]
        lanes = slice(k * PATCHES, (k + 1) * PATCHES)
        ohn_ref[:, lanes] = one_hot(ids & 127, 128).astype(BF)
        maskn_ref[:, lanes] = one_hot(ids >> 7, 8)
    for q in range(4):
        ids = conn_ref[q : q + 1, :]
        ids = jnp.where(ids >= HS, ids - HS, ids + (S + 128 - HS))
        lanes = slice(q * SE, (q + 1) * SE)
        ohc_ref[:, lanes] = one_hot(ids & 127, 128).astype(BF)
        maskc_ref[:, lanes] = one_hot(ids >> 7, 8)
        mask8_ref[:, lanes] = ((ids >> 7) == 8).astype(F32)

    def internal(step):
        lane = iota((8, 128), 1)
        from_right = rim_ref[step, 0] * jnp.where(dom < N_DOM - 1, 1.0, 0.0)
        from_left = rim_ref[step, 1] * jnp.where(dom > 0, 1.0, 0.0)
        rim = jnp.where(lane < 64, from_right, from_left)
        read = joined(dot(halves(jnp.concatenate([d_ref[...], rim], axis=0)), ohc_ref[...]))
        picked = []
        for c in range(3):
            values = jnp.sum(read[c * 8 : c * 8 + 8] * maskc_ref[...], axis=0, keepdims=True)
            values = values + read[24 + c : 25 + c] * mask8_ref[...]
            picked += [values[:, q * SE : (q + 1) * SE] for q in range(4)]
        force = jnp.dot(
            stiff_ref[...], jnp.concatenate(picked, axis=0), precision=HIGHEST, preferred_element_type=F32
        )
        force = force * scale_ref[...]
        spread = []
        for c in range(3):
            line_c = jnp.concatenate([force[c * 4 + q : c * 4 + q + 1] for q in range(4)], axis=1)
            spread.append(line_c * maskc_ref[...])
        return joined(dot_t(halves(jnp.concatenate(spread, axis=0)), ohc_ref[...]))

    for c in rim0:
        c.wait()
    inner = internal(0)

    for c in flow:
        c.wait()
    early = [copy(wsend_ref.at[d], wrecv_ref.at[d], w_s.at[d], w_r.at[d], dom_peer(d)) for d in range(1, N_DOM)]
    for c in early:
        c.start()
    wrecv_ref[0] = wsend_ref[0]
    keep_hi = jnp.where(line < devices - 1, 1.0, 0.0).astype(BF)
    keep_lo = jnp.where(line > 0, 1.0, 0.0).astype(BF)
    extract(lambda w: hhi_ref[w * 128 : w * 128 + 128, :] * keep_hi, PARTS - 1, slice(0, HALO))
    extract(lambda w: hlo_ref[w * 128 : w * 128 + 128, :] * keep_lo, PARTS - 1, slice(HALO, 2 * HALO))

    def neighbour(face, ids):
        ids = jnp.where(ids >= HALO, ids - HALO, ids + (E + HALO))
        picked = dot(src_ref[face], one_hot(ids & (PART - 1), PART).astype(BF))
        part = ids // PART
        other = picked[0:128]
        for p in range(1, PARTS):
            other = jnp.where(part == p, picked[p * 128 : p * 128 + 128], other)
        return other.astype(BF)

    for half in range(F // TILE):
        cols = slice(half * TILE, (half + 1) * TILE)
        for face in range(6):
            surf_ref[face * 128 : face * 128 + 128, cols] = neighbour(face, surf_near[face : face + 1, cols])
    found = base + surf_factor * dot(ab_ref[last, ROWS:DEPTH], surf_ref[...])
    found = found.astype(BF).astype(F32)
    pressure = jnp.sum(jnp.where(iota((128, F), 0) == snode_ref[...], found, 0.0), axis=0, keepdims=True)
    traction = jnp.concatenate([normal_ref[...] * pressure, jnp.zeros((5, F), F32)], axis=0)
    rows = jnp.concatenate([traction * owned[d : d + 1] for d in range(N_DOM)], axis=0)
    tsend_ref[...] = joined(dot_t(halves(rows), ohs_ref[...])).reshape(N_DOM, 8, CAP)
    loads = [copy(tsend_ref.at[d], trecv_ref.at[d], t_s.at[d], t_r.at[d], dom_peer(d)) for d in range(1, N_DOM)]
    for c in loads:
        c.start()
    trecv_ref[0] = tsend_ref[0]

    def advance(t, carry):
        cols = pl.ds(pl.multiple_of(t * TILE, TILE), TILE)
        for face in range(6):
            x_ref[ROWS + face * 128 : ROWS + face * 128 + 128, cols] = neighbour(face, nb_ref[face : face + 1, cols])
        factor = FLOW_STEP * jac_ref[:, cols]
        change = dot(ab_ref[...], x_ref[:, cols])
        for v in range(VARS):
            moved = x_ref[v * 128 : v * 128 + 128, cols].astype(F32) + factor * change[v * 128 : v * 128 + 128]
            fluid_ref[v, :, cols] = moved.astype(BF)[:NP]
        return carry

    tiles = (2, 2, 2, 2)

    def fill(wait):
        lax.fori_loop(sum(tiles[:wait]), sum(tiles[: wait + 1]), advance, 0)

    for c in early:
        c.wait()
    for d in range(N_DOM):
        block = wrecv_ref[d].astype(F32)
        wall_ref[:, d * CAP : (d + 1) * CAP] = block[0:K]
        ohp_ref[:, d * CAP : (d + 1) * CAP] = one_hot(block[K : K + 1].astype(I32), PATCHES).astype(BF)
    fill(0)

    for c in loads:
        c.wait()
    load = []
    for c in range(3):
        line_c = jnp.concatenate([trecv_ref[d, c : c + 1, :] for d in range(N_DOM)], axis=1)
        load.append(wall_ref[...] * line_c)
    by_patch = joined(dot_t(halves(jnp.concatenate(load, axis=0)), ohp_ref[...]))
    spread = []
    for c in range(3):
        line_c = jnp.concatenate([by_patch[c * K + k : c * K + k + 1] for k in range(K)], axis=1)
        spread.append(line_c * maskn_ref[...])
    partial = joined(dot_t(halves(jnp.concatenate(spread, axis=0)), ohn_ref[...]))
    ebuf_ref[...] = partial
    sums = [copy(ebuf_ref, erecv_ref.at[d], e_s.at[d], e_r.at[d], sec_peer(d)) for d in range(1, N_SEC)]
    for c in sums:
        c.start()
    erecv_ref[0] = partial
    fill(1)
    for c in sums:
        c.wait()
    external = erecv_ref[lax.rem(sec, N_SEC)]
    for s in range(1, N_SEC):
        external = external + erecv_ref[lax.rem(sec - s + N_SEC, N_SEC)]

    mass = jnp.concatenate([m_ref[...]] * 3, axis=0)
    for step in range(STEPS):
        if step > 0:
            edges(step)
            around = rims(step)
            for c in around:
                c.start()
            fill(2)
            for c in around:
                c.wait()
            inner = internal(step)
        velocity = v_ref[...] + SHELL_STEP * mass * (external - inner)
        v_ref[...] = velocity
        d_ref[...] = d_ref[...] + SHELL_STEP * velocity

    read = joined(dot(halves(d_ref[...]), ohn_ref[...]))
    nodes = []
    for c in range(3):
        values = jnp.sum(read[c * 8 : c * 8 + 8] * maskn_ref[...], axis=0, keepdims=True)
        nodes += [values[:, k * PATCHES : (k + 1) * PATCHES] for k in range(K)]
    by_row = joined(dot(halves(jnp.concatenate(nodes, axis=0)), ohp_ref[...]))
    rsend_ref[...] = jnp.zeros(rsend_ref.shape, F32)
    for c in range(3):
        total = jnp.sum(by_row[c * K : (c + 1) * K] * wall_ref[...], axis=0, keepdims=True)
        for d in range(N_DOM):
            rsend_ref[d, c : c + 1, :] = total[:, d * CAP : (d + 1) * CAP]
    returns = [
        copy(rsend_ref.at[d], rrecv_ref.at[d], r_s.at[d], r_r.at[d], dom_peer(N_DOM - d)) for d in range(1, N_DOM)
    ]
    for c in returns:
        c.start()
    rrecv_ref[0] = rsend_ref[0]
    for h in range(8):
        for c in range(3):
            shell_ref[c : c + 1, h * 128 : (h + 1) * 128] = d_ref[c * 8 + h : c * 8 + h + 1, :]
    fill(3)
    for c in returns:
        c.wait()
    back = joined(dot(halves(rrecv_ref[...].reshape(N_DOM * 8, CAP)), ohs_ref[...]))
    shift = back[0:8] * owned[0:1]
    for d in range(1, N_DOM):
        shift = shift + back[d * 8 : d * 8 + 8] * owned[d : d + 1]
    shift_ref[...] = shift[0:3]


def on_device(
    fluid_state, jac_inv, flux_mats, neighbours, surf_elem, surf_node, normals, rbf_weights, owners,
    patches, patch_nodes, shell_disp, shell_vel, mass_inv, shell_conn, elem_scale, elem_stiff,
):
    own, select, place = constants()
    vmem, hbm = pl.BlockSpec(memory_space=pltpu.VMEM), pl.BlockSpec(memory_space=pl.ANY)
    dma = pltpu.SemaphoreType.DMA
    return pl.pallas_call(
        kernel,
        out_shape=(
            pltpu.VMEM((VARS, NP, E), BF),
            pltpu.VMEM((3, S), F32),
            pltpu.VMEM((3, F), F32),
        ),
        in_specs=[hbm] + [vmem] * 16 + [hbm] * 3,
        out_specs=(vmem, vmem, vmem),
        scratch_shapes=[
            pltpu.VMEM((VARS, NP, E), BF),
            pltpu.VMEM((4, 128, 128), F32),
            pltpu.VMEM((VARS, 6 * 32, 128), BF),
            pltpu.VMEM((6, 128, 128), BF),
            pltpu.VMEM((DEPTH, E), BF),
            pltpu.VMEM((6, PARTS * 128, PART), BF),
            pltpu.VMEM((ROWS, DEPTH), BF),
            pltpu.VMEM((ROWS, HALO), BF),
            pltpu.VMEM((ROWS, HALO), BF),
            pltpu.VMEM((6 * 128, F), BF),
            pltpu.VMEM((PATCHES, N_DOM * CAP), BF),
            pltpu.VMEM((128, K * PATCHES), BF),
            pltpu.VMEM((8, K * PATCHES), F32),
            pltpu.VMEM((128, 4 * SE), BF),
            pltpu.VMEM((8, 4 * SE), F32),
            pltpu.VMEM((1, 4 * SE), F32),
            pltpu.VMEM((CAP, F), BF),
            pltpu.VMEM((N_DOM, 32, CAP), BF),
            pltpu.VMEM((N_DOM, 32, CAP), BF),
            pltpu.VMEM((K, N_DOM * CAP), F32),
            pltpu.VMEM((N_DOM, 8, CAP), F32),
            pltpu.VMEM((N_DOM, 8, CAP), F32),
            pltpu.VMEM((N_DOM, 8, CAP), F32),
            pltpu.VMEM((N_DOM, 8, CAP), F32),
            pltpu.VMEM((24, 128), F32),
            pltpu.VMEM((N_SEC, 24, 128), F32),
            pltpu.VMEM((STEPS, 2, 8, 128), F32),
            pltpu.VMEM((STEPS, 2, 8, 128), F32),
            pltpu.VMEM((24, 128), F32),
            pltpu.VMEM((24, 128), F32),
            pltpu.VMEM((8, 128), F32),
            dma((4,)), dma((2,)), dma((2,)),
            dma((N_DOM,)), dma((N_DOM,)),
            dma((N_DOM,)), dma((N_DOM,)),
            dma((N_DOM,)), dma((N_DOM,)),
            dma((N_SEC,)), dma((N_SEC,)),
            dma((STEPS, 2)), dma((STEPS, 2)),
        ],
        compiler_params=pltpu.CompilerParams(
            collective_id=0, has_side_effects=True, vmem_limit_bytes=56 * 1024 * 1024
        ),
    )(
        fluid_state, jac_inv.reshape(1, E), jnp.transpose(flux_mats, (1, 0, 2)), neighbours, surf_elem.reshape(1, F),
        surf_node.reshape(1, F), normals, rbf_weights, owners.reshape(1, F), patches.reshape(1, F),
        patch_nodes, shell_disp, shell_vel, mass_inv.reshape(1, S), shell_conn,
        elem_scale.reshape(1, SE), elem_stiff, jnp.asarray(own), jnp.asarray(select), jnp.asarray(place),
    )


def solution(mesh):
    flow, shell = ("sec", "dom"), "dom"
    return jax.shard_map(
        on_device,
        mesh=mesh,
        in_specs=(
            P(None, None, flow),
            P(flow),
            P(),
            P(None, flow),
            P(flow),
            P(flow),
            P(None, flow),
            P(None, flow),
            P(flow, None),
            P(flow),
            P(None, shell),
            P(None, shell),
            P(None, shell),
            P(shell),
            P(None, shell),
            P(shell),
            P(),
        ),
        out_specs=(P(None, None, flow), P(None, shell), P(None, flow)),
        check_vma=False,
    )
```

```python
import jax
import jax.numpy as jnp
import numpy as np
from jax import lax
from jax.experimental import pallas as pl
from jax.experimental.pallas import tpu as pltpu
from jax.sharding import PartitionSpec as P

VARS, NP, K, STEPS = 5, 125, 16, 2
E, F, PATCHES, S, SE = 2048, 512, 256, 1024, 1024
HALO, HS, CAP = 256, 32, 128
N_SEC, N_DOM = 8, 16
LIFT, _STEP, SHELL_STEP = 10.0, 0.02, 0.3

TILE = 256
PART = 512
PARTS = (E + 2 * HALO) // PART
ROWS = VARS * 128
DEPTH = ROWS + 6 * 128
BF, F32, I32 = jnp.bfloat16, jnp.float32, jnp.int32
HIGHEST = lax.Precision.HIGHEST
MESH = pl.DeviceIdType.MESH


def lgl_derivative():
    points = np.array([-1.0, -np.sqrt(3.0 / 7.0), 0.0, np.sqrt(3.0 / 7.0), 1.0])
    barycentric = np.array(
        [
            1.0 / np.prod([points[col] - points[other] for other in range(5) if other != col])
            for col in range(5)
        ]
    )
    derivative = np.zeros((5, 5))
    for row in range(5):
        for col in range(5):
            if row != col:
                derivative[row, col] = (
                    barycentric[col] / barycentric[row] / (points[row] - points[col])
                )
        derivative[row, row] = -np.sum(derivative[row])
    return derivative.astype(np.float32)


def constants():
    nodes = np.arange(NP).reshape(5, 5, 5)
    faces = [nodes[0], nodes[4], nodes[:, 0], nodes[:, 4], nodes[:, :, 0], nodes[:, :, 4]]
    faces = [face.reshape(25) for face in faces]
    d, eye = lgl_derivative(), np.eye(5, dtype=np.float32)
    own = np.zeros((4, 128, 128), np.float32)
    own[0, :NP, :NP] = -np.kron(np.kron(d, eye), eye)
    own[1, :NP, :NP] = -np.kron(np.kron(eye, d), eye)
    own[2, :NP, :NP] = -np.kron(np.kron(eye, eye), d)
    for face in range(6):
        sign = 1.0 if face % 2 else -1.0
        for node in faces[face]:
            own[face // 2, node, node] += sign * 0.5 * LIFT
            own[3, node, node] -= 0.5 * LIFT
    select = np.zeros((VARS, 6 * 32, 128), np.float32)
    place = np.zeros((6, 128, 128), np.float32)
    for face in range(6):
        for n in range(25):
            for w in range(VARS):
                select[w, face * 32 + w + n, faces[face ^ 1][n]] = 1.0
                place[face, faces[face][n], 25 * w + n] = -0.5 * LIFT
    return own, select.astype(jnp.bfloat16), place.astype(jnp.bfloat16)


def dot(a, b):
    return jnp.dot(a, b, preferred_element_type=F32)


def dot_t(a, b):
    return lax.dot_general(a, b, (((1,), (1,)), ((), ())), preferred_element_type=F32)


def halves(x):
    high = x.astype(BF)
    low = (x - high.astype(F32)).astype(BF)
    return jnp.concatenate([high, low], axis=0)


def joined(y):
    rows = y.shape[0] // 2
    return y[:rows] + y[rows:]


def iota(shape, dim):
    return lax.broadcasted_iota(I32, shape, dim)


def one_hot(ids, rows):
    return (iota((rows, ids.shape[1]), 0) == ids).astype(F32)


def kernel(
    state_ref, jac_ref, flux_ref, nb_ref, selem_ref, snode_ref, normal_ref, weight_ref, owner_ref,
    patch_ref, pnode_ref, disp_ref, vel_ref, minv_ref, conn_ref, scale_ref, stiff_ref,
    own_hbm, select_hbm, place_hbm,
    fluid_ref, shell_ref, shift_ref,
    u_ref, own_ref, select_ref, place_ref, x_ref, src_ref, ab_ref, hlo_ref, hhi_ref,
    g_ref, gsend_ref, grecv_ref, ohp_ref, ohn_ref, maskn_ref, ohc_ref, maskc_ref, mask8_ref, ohs_ref,
    wsend_ref, wrecv_ref, wall_ref, tsend_ref, trecv_ref, rsend_ref, rrecv_ref,
    ebuf_ref, erecv_ref, edge_ref, rim_ref, d_ref, v_ref, m_ref,
    local_s, g_s, g_r, flow_s, flow_r, w_s, w_r, t_s, t_r, r_s, r_r, e_s, e_r, rim_s, rim_r,
):
    sec, dom = lax.axis_index("sec"), lax.axis_index("dom")
    line = sec * N_DOM + dom
    devices = N_SEC * N_DOM
    nxt, prv = lax.rem(line + 1, devices), lax.rem(line + devices - 1, devices)
    right = (nxt // N_DOM, lax.rem(nxt, N_DOM))
    left = (prv // N_DOM, lax.rem(prv, N_DOM))

    def dom_peer(d):
        return (sec, lax.rem(dom + d, N_DOM))

    def sec_peer(d):
        return (lax.rem(sec + d, N_SEC), dom)

    def copy(src, dst, send, recv, device):
        return pltpu.make_async_remote_copy(
            src_ref=src, dst_ref=dst, send_sem=send, recv_sem=recv, device_id=device, device_id_type=MESH
        )

    def all_of(src, dst, send, recv):
        return copy(src.at[1 : src.shape[0]], dst.at[1 : dst.shape[0]], send.at[0], recv.at[0], dom_peer(1))

    barrier = pltpu.get_barrier_semaphore()
    greeted = [dom_peer(d) for d in range(1, N_DOM)] + [sec_peer(d) for d in range(1, N_SEC)] + [right, left]
    for device in greeted:
        pl.semaphore_signal(barrier, inc=1, device_id=device, device_id_type=MESH)

    fetch = [
        pltpu.make_async_copy(src, dst, local_s.at[i])
        for i, (src, dst) in enumerate(
            ((state_ref, u_ref), (own_hbm, own_ref), (select_hbm, select_ref), (place_hbm, place_ref))
        )
    ]
    for c in fetch:
        c.start()

    for h in range(8):
        lanes = slice(h * 128, (h + 1) * 128)
        m_ref[h : h + 1, :] = minv_ref[:, lanes]
        for c in range(3):
            d_ref[c * 8 + h : c * 8 + h + 1, :] = disp_ref[c : c + 1, lanes]
            v_ref[c * 8 + h : c * 8 + h + 1, :] = vel_ref[c : c + 1, lanes]

    def edges(step):
        for c in range(3):
            edge_ref[step, 0, c : c + 1, :] = d_ref[c * 8 : c * 8 + 1, :]
            edge_ref[step, 1, c : c + 1, :] = d_ref[c * 8 + 7 : c * 8 + 8, :]

    def rims(step):
        return [
            copy(edge_ref.at[step, 0], rim_ref.at[step, 0], rim_s.at[step, 0], rim_r.at[step, 0], dom_peer(N_DOM - 1)),
            copy(edge_ref.at[step, 1], rim_ref.at[step, 1], rim_s.at[step, 1], rim_r.at[step, 1], dom_peer(1)),
        ]

    edge_ref[...] = jnp.zeros(edge_ref.shape, F32)
    edges(0)

    relative = (owner_ref[...] - dom + N_DOM) & (N_DOM - 1)
    owned = one_hot(relative, N_DOM)
    earlier = (iota((F, F), 0) < iota((F, F), 1)).astype(F32).astype(BF)
    rank = jnp.sum(owned * dot(owned.astype(BF), earlier), axis=0, keepdims=True).astype(I32)
    ohs_ref[...] = one_hot(rank, CAP).astype(BF)

    penalty = None
    for v in range(VARS):
        total = jnp.max(jnp.sum(jnp.abs(flux_ref[v]), axis=1, keepdims=True), axis=0, keepdims=True)
        penalty = total if penalty is None else jnp.maximum(penalty, total)

    def flux(d, v, w):
        return flux_ref[v, d : d + 1, w : w + 1]


    def coupling(face, v, w):
        value = (1.0 if face % 2 else -1.0) * flux(face // 2, v, w)
        return value - penalty if v == w else value

    fetch[0].wait()
    for v in range(VARS):
        x_ref[v * 128 + 112 : v * 128 + 128, :] = jnp.zeros((16, E), BF)
        x_ref[v * 128 : v * 128 + NP, :] = u_ref[v]

    for c in fetch[1:]:
        c.wait()
    choice = select_ref[0].astype(F32) * (-0.5 * LIFT)
    couple = []
    for w in range(VARS):
        blocks = [choice[face * 32 : face * 32 + 32] * coupling(face, VARS - 1, w) for face in range(6)]
        couple.append(jnp.concatenate(blocks, axis=0).astype(BF))
    couple = jnp.concatenate(couple, axis=1)
    gsend_ref[0] = dot(couple, x_ref[0:ROWS, E - HALO : E]).astype(BF)
    gsend_ref[1] = dot(couple, x_ref[0:ROWS, 0:HALO]).astype(BF)

    pl.semaphore_wait(barrier, len(greeted))
    first = [
        copy(gsend_ref.at[0], grecv_ref.at[0], g_s.at[0], g_r.at[0], right),
        copy(gsend_ref.at[1], grecv_ref.at[1], g_s.at[1], g_r.at[1], left),
    ]
    for c in first:
        c.start()
    rim0 = rims(0)
    for c in rim0:
        c.start()
    flow = [
        copy(x_ref.at[0:ROWS, E - HALO : E], hlo_ref, flow_s.at[0], flow_r.at[0], right),
        copy(x_ref.at[0:ROWS, 0:HALO], hhi_ref, flow_s.at[1], flow_r.at[1], left),
    ]

    for c in flow:
        c.start()

    def spread_faces(values, part):
        for face in range(6):
            g_ref[face, part * 32 : part * 32 + 32, :] = values[face * 32 : face * 32 + 32]

    def operator(v):
        for w in range(VARS):
            block = flux(0, v, w) * own_ref[0] + flux(1, v, w) * own_ref[1] + flux(2, v, w) * own_ref[2]
            if v == w:
                block = block + penalty * own_ref[3]
            ab_ref[v * 128 : v * 128 + 128, w * 128 : w * 128 + 128] = block.astype(BF)

    operator(VARS - 1)

    last = slice((VARS - 1) * 128, VARS * 128)
    elems = selem_ref[...]
    picker = one_hot(elems & (TILE - 1), TILE).astype(BF)
    base, near = jnp.zeros((128, F), F32), jnp.zeros((16, F), F32)
    for h in range(E // TILE):
        cols = slice(h * TILE, (h + 1) * TILE)
        factor = _STEP * jac_ref[:, cols]
        spread_faces(dot(couple, x_ref[0:ROWS, cols]).astype(BF), h + 1)
        moved = x_ref[last, cols].astype(F32) + factor * dot(ab_ref[last, 0:ROWS], x_ref[0:ROWS, cols])
        ids = nb_ref[:, cols]
        rows = jnp.concatenate(
            [halves(factor), (ids & 255).astype(F32).astype(BF), (ids >> 8).astype(F32).astype(BF)], axis=0
        )
        rows = jnp.concatenate([halves(moved), rows, jnp.zeros((2, TILE), BF)], axis=0)
        found = dot(rows, picker)
        mine = (elems // TILE) == h
        base = jnp.where(mine, joined(found[0:256]), base)
        near = jnp.where(mine, found[256:272], near)
    surf_factor = near[0:1] + near[1:2]
    column_of, block_of = near[2:8].astype(I32), near[8:14].astype(I32)

    payload = jnp.concatenate([weight_ref[...], patch_ref[...].astype(F32), jnp.zeros((15, F), F32)], axis=0)
    payload = jnp.concatenate([payload * owned[d : d + 1] for d in range(N_DOM)], axis=0)
    placed = dot_t(payload.astype(BF), ohs_ref[...])
    wsend_ref[...] = placed.astype(BF).reshape(N_DOM, 32, CAP)

    early = [copy(wsend_ref.at[d], wrecv_ref.at[d], w_s.at[0], w_r.at[0], dom_peer(d)) for d in range(1, N_DOM)]
    for c in early:
        c.start()
    wrecv_ref[0] = wsend_ref[0]

    for k in range(K):
        ids = pnode_ref[k : k + 1, :]
        lanes = slice(k * PATCHES, (k + 1) * PATCHES)
        ohn_ref[:, lanes] = one_hot(ids & 127, 128).astype(BF)
        maskn_ref[:, lanes] = one_hot(ids >> 7, 8)
    for v in range(VARS - 1):
        operator(v)
    column = iota((1, 128), 1)
    for face in range(6):
        where = place_ref[face].astype(F32)
        for v in range(VARS):
            factor = jnp.zeros((1, 128), F32)
            for w in range(VARS):
                factor = jnp.where((column >= 25 * w) & (column < 25 * w + 25), coupling(face, v, w), factor)
            ab_ref[v * 128 : v * 128 + 128, ROWS + face * 128 : ROWS + face * 128 + 128] = (where * factor).astype(BF)

    for c in first:
        c.wait()
    keep_hi = jnp.where(line < devices - 1, 1.0, 0.0).astype(BF)
    keep_lo = jnp.where(line > 0, 1.0, 0.0).astype(BF)
    spread_faces(grecv_ref[0] * keep_lo, 0)
    spread_faces(grecv_ref[1] * keep_hi, E // HALO + 1)
    n = iota((32, F), 0)
    i, j = (n * 13) >> 6, n - 5 * ((n * 13) >> 6)
    added = jnp.zeros((32, F), F32)
    for face in range(6):
        picked = dot(g_ref[face], one_hot(column_of[face : face + 1], HALO).astype(BF))
        block = block_of[face : face + 1]
        other = picked[0:32]
        for p in range(1, E // HALO + 2):
            other = jnp.where(block == p, picked[p * 32 : p * 32 + 32], other)
        node = (n, n + 100, 25 * i + j, 25 * i + j + 20, 5 * n, 5 * n + 4)[face]
        added = added + jnp.where((node == snode_ref[...]) & (n < 25), other, 0.0)
    own_part = jnp.sum(jnp.where(iota((128, F), 0) == snode_ref[...], base, 0.0), axis=0, keepdims=True)
    pressure = own_part + surf_factor * jnp.sum(added, axis=0, keepdims=True)
    pressure = pressure.astype(BF).astype(F32)
    traction = jnp.concatenate([normal_ref[...] * pressure, jnp.zeros((5, F), F32)], axis=0)
    rows = jnp.concatenate([traction * owned[d : d + 1] for d in range(N_DOM)], axis=0)
    tsend_ref[...] = joined(dot_t(halves(rows), ohs_ref[...])).reshape(N_DOM, 8, CAP)
    loads = [copy(tsend_ref.at[d], trecv_ref.at[d], t_s.at[0], t_r.at[0], dom_peer(d)) for d in range(1, N_DOM)]
    for c in loads:
        c.start()
    trecv_ref[0] = tsend_ref[0]

    def neighbour(face, ids):
        ids = jnp.where(ids >= HALO, ids - HALO, ids + (E + HALO))
        picked = dot(src_ref[face], one_hot(ids & (PART - 1), PART).astype(BF))
        part = ids // PART
        other = picked[0:128]
        for p in range(1, PARTS):
            other = jnp.where(part == p, picked[p * 128 : p * 128 + 128], other)
        return other.astype(BF)

    def advance(t, carry):
        cols = pl.ds(pl.multiple_of(t * TILE, TILE), TILE)
        for face in range(6):
            x_ref[ROWS + face * 128 : ROWS + face * 128 + 128, cols] = neighbour(face, nb_ref[face : face + 1, cols])
        factor = _STEP * jac_ref[:, cols]
        change = dot(ab_ref[...], x_ref[:, cols])
        for v in range(VARS):
            moved = x_ref[v * 128 : v * 128 + 128, cols].astype(F32) + factor * change[v * 128 : v * 128 + 128]
            fluid_ref[v, :, cols] = moved.astype(BF)[:NP]
        return carry

    tiles = (0, 3, 2, 3)

    def fill(wait):
        lax.fori_loop(sum(tiles[:wait]), sum(tiles[: wait + 1]), advance, 0, unroll=True)

    def extract(values, part, lanes):
        e = [dot(select_ref[w], values(w)) for w in range(VARS)]
        for face in range(6):
            g = [x[face * 32 : face * 32 + 32] for x in e]
            pieces = [g[0][0:24]]
            for w in range(1, VARS):
                pieces += [g[w - 1][24:32] + g[w][0:8], g[w][8:24]]
            pieces += [g[VARS - 1][24:32]]
            src_ref[face, pl.ds(part * 128, 128), lanes] = jnp.concatenate(pieces, axis=0).astype(BF)

    for part in range(E // PART):
        for half in range(PART // TILE):
            cols = slice(part * PART + half * TILE, part * PART + (half + 1) * TILE)
            extract(lambda w: x_ref[w * 128 : w * 128 + 128, cols], part, slice(half * TILE, (half + 1) * TILE))

    def internal(step):
        lane = iota((8, 128), 1)
        from_right = rim_ref[step, 0] * jnp.where(dom < N_DOM - 1, 1.0, 0.0)
        from_left = rim_ref[step, 1] * jnp.where(dom > 0, 1.0, 0.0)
        rim = jnp.where(lane < 64, from_right, from_left)
        read = joined(dot(halves(jnp.concatenate([d_ref[...], rim], axis=0)), ohc_ref[...]))
        picked = []
        for c in range(3):
            values = jnp.sum(read[c * 8 : c * 8 + 8] * maskc_ref[...], axis=0, keepdims=True)
            values = values + read[24 + c : 25 + c] * mask8_ref[...]
            picked += [values[:, q * SE : (q + 1) * SE] for q in range(4)]
        force = jnp.dot(
            stiff_ref[...], jnp.concatenate(picked, axis=0), precision=HIGHEST, preferred_element_type=F32
        )
        force = force * scale_ref[...]
        spread = []
        for c in range(3):
            line_c = jnp.concatenate([force[c * 4 + q : c * 4 + q + 1] for q in range(4)], axis=1)
            spread.append(line_c * maskc_ref[...])
        return joined(dot_t(halves(jnp.concatenate(spread, axis=0)), ohc_ref[...]))

    for q in range(4):
        ids = conn_ref[q : q + 1, :]
        ids = jnp.where(ids >= HS, ids - HS, ids + (S + 128 - HS))
        lanes = slice(q * SE, (q + 1) * SE)
        ohc_ref[:, lanes] = one_hot(ids & 127, 128).astype(BF)
        maskc_ref[:, lanes] = one_hot(ids >> 7, 8)
        mask8_ref[:, lanes] = ((ids >> 7) == 8).astype(F32)

    for c in rim0:
        c.wait()
    inner = internal(0)

    all_of(wsend_ref, wrecv_ref, w_s, w_r).wait()
    for d in range(N_DOM):
        block = wrecv_ref[d].astype(F32)
        wall_ref[:, d * CAP : (d + 1) * CAP] = block[0:K]
        ohp_ref[:, d * CAP : (d + 1) * CAP] = one_hot(block[K : K + 1].astype(I32), PATCHES).astype(BF)
    fill(0)

    all_of(tsend_ref, trecv_ref, t_s, t_r).wait()
    load = []
    for c in range(3):
        line_c = jnp.concatenate([trecv_ref[d, c : c + 1, :] for d in range(N_DOM)], axis=1)
        load.append(wall_ref[...] * line_c)
    by_patch = joined(dot_t(halves(jnp.concatenate(load, axis=0)), ohp_ref[...]))
    spread = []
    for c in range(3):
        line_c = jnp.concatenate([by_patch[c * K + k : c * K + k + 1] for k in range(K)], axis=1)
        spread.append(line_c * maskn_ref[...])
    partial = joined(dot_t(halves(jnp.concatenate(spread, axis=0)), ohn_ref[...]))
    ebuf_ref[...] = partial
    sums = [copy(ebuf_ref, erecv_ref.at[d], e_s.at[0], e_r.at[0], sec_peer(d)) for d in range(1, N_SEC)]
    for c in sums:
        c.start()
    erecv_ref[0] = partial

    for c in flow:
        c.wait()
    extract(lambda w: hhi_ref[w * 128 : w * 128 + 128, :] * keep_hi, PARTS - 1, slice(0, HALO))
    extract(lambda w: hlo_ref[w * 128 : w * 128 + 128, :] * keep_lo, PARTS - 1, slice(HALO, 2 * HALO))
    fill(1)
    all_of(erecv_ref, erecv_ref, e_s, e_r).wait()
    external = erecv_ref[lax.rem(sec, N_SEC)]
    for s in range(1, N_SEC):
        external = external + erecv_ref[lax.rem(sec - s + N_SEC, N_SEC)]

    mass = jnp.concatenate([m_ref[...]] * 3, axis=0)
    for step in range(STEPS):
        if step > 0:
            edges(step)
            around = rims(step)
            for c in around:
                c.start()
            fill(2)
            for c in around:
                c.wait()
            inner = internal(step)
        velocity = v_ref[...] + SHELL_STEP * mass * (external - inner)
        v_ref[...] = velocity
        d_ref[...] = d_ref[...] + SHELL_STEP * velocity

    read = joined(dot(halves(d_ref[...]), ohn_ref[...]))
    nodes = []
    for c in range(3):
        values = jnp.sum(read[c * 8 : c * 8 + 8] * maskn_ref[...], axis=0, keepdims=True)
        nodes += [values[:, k * PATCHES : (k + 1) * PATCHES] for k in range(K)]
    by_row = joined(dot(halves(jnp.concatenate(nodes, axis=0)), ohp_ref[...]))
    rsend_ref[...] = jnp.zeros(rsend_ref.shape, F32)
    for c in range(3):
        total = jnp.sum(by_row[c * K : (c + 1) * K] * wall_ref[...], axis=0, keepdims=True)
        for d in range(N_DOM):
            rsend_ref[d, c : c + 1, :] = total[:, d * CAP : (d + 1) * CAP]
    returns = [
        copy(rsend_ref.at[d], rrecv_ref.at[d], r_s.at[0], r_r.at[0], dom_peer(N_DOM - d)) for d in range(1, N_DOM)
    ]
    for c in returns:
        c.start()
    rrecv_ref[0] = rsend_ref[0]
    for h in range(8):
        for c in range(3):
            shell_ref[c : c + 1, h * 128 : (h + 1) * 128] = d_ref[c * 8 + h : c * 8 + h + 1, :]
    fill(3)
    all_of(rsend_ref, rrecv_ref, r_s, r_r).wait()
    back = joined(dot(halves(rrecv_ref[...].reshape(N_DOM * 8, CAP)), ohs_ref[...]))
    shift = back[0:8] * owned[0:1]
    for d in range(1, N_DOM):
        shift = shift + back[d * 8 : d * 8 + 8] * owned[d : d + 1]
    shift_ref[...] = shift[0:3]


def on_device(
    fluid_state, jac_inv, flux_mats, neighbours, surf_elem, surf_node, normals, rbf_weights, owners,
    patches, patch_nodes, shell_disp, shell_vel, mass_inv, shell_conn, elem_scale, elem_stiff,
):
    own, select, place = constants()
    vmem, hbm = pl.BlockSpec(memory_space=pltpu.VMEM), pl.BlockSpec(memory_space=pl.ANY)
    dma = pltpu.SemaphoreType.DMA
    return pl.pallas_call(
        kernel,
        out_shape=(
            pltpu.VMEM((VARS, NP, E), BF),
            pltpu.VMEM((3, S), F32),
            pltpu.VMEM((3, F), F32),
        ),
        in_specs=[hbm] + [vmem] * 16 + [hbm] * 3,
        out_specs=(vmem, vmem, vmem),
        scratch_shapes=[
            pltpu.VMEM((VARS, NP, E), BF),
            pltpu.VMEM((4, 128, 128), F32),
            pltpu.VMEM((VARS, 6 * 32, 128), BF),
            pltpu.VMEM((6, 128, 128), BF),
            pltpu.VMEM((DEPTH, E), BF),
            pltpu.VMEM((6, PARTS * 128, PART), BF),
            pltpu.VMEM((ROWS, DEPTH), BF),
            pltpu.VMEM((ROWS, HALO), BF),
            pltpu.VMEM((ROWS, HALO), BF),
            pltpu.VMEM((6, (E // HALO + 2) * 32, HALO), BF),
            pltpu.VMEM((2, 6 * 32, HALO), BF),
            pltpu.VMEM((2, 6 * 32, HALO), BF),
            pltpu.VMEM((PATCHES, N_DOM * CAP), BF),
            pltpu.VMEM((128, K * PATCHES), BF),
            pltpu.VMEM((8, K * PATCHES), F32),
            pltpu.VMEM((128, 4 * SE), BF),
            pltpu.VMEM((8, 4 * SE), F32),
            pltpu.VMEM((1, 4 * SE), F32),
            pltpu.VMEM((CAP, F), BF),
            pltpu.VMEM((N_DOM, 32, CAP), BF),
            pltpu.VMEM((N_DOM, 32, CAP), BF),
            pltpu.VMEM((K, N_DOM * CAP), F32),
            pltpu.VMEM((N_DOM, 8, CAP), F32),
            pltpu.VMEM((N_DOM, 8, CAP), F32),
            pltpu.VMEM((N_DOM, 8, CAP), F32),
            pltpu.VMEM((N_DOM, 8, CAP), F32),
            pltpu.VMEM((24, 128), F32),
            pltpu.VMEM((N_SEC, 24, 128), F32),
            pltpu.VMEM((STEPS, 2, 8, 128), F32),
            pltpu.VMEM((STEPS, 2, 8, 128), F32),
            pltpu.VMEM((24, 128), F32),
            pltpu.VMEM((24, 128), F32),
            pltpu.VMEM((8, 128), F32),
            dma((4,)), dma((2,)), dma((2,)), dma((2,)), dma((2,)),
            dma((1,)), dma((1,)),
            dma((1,)), dma((1,)),
            dma((1,)), dma((1,)),
            dma((1,)), dma((1,)),
            dma((STEPS, 2)), dma((STEPS, 2)),
        ],
        compiler_params=pltpu.CompilerParams(
            collective_id=0, has_side_effects=True, vmem_limit_bytes=56 * 1024 * 1024
        ),
    )(
        fluid_state, jac_inv.reshape(1, E), jnp.transpose(flux_mats, (1, 0, 2)), neighbours, surf_elem.reshape(1, F),
        surf_node.reshape(1, F), normals, rbf_weights, owners.reshape(1, F), patches.reshape(1, F),
        patch_nodes, shell_disp, shell_vel, mass_inv.reshape(1, S), shell_conn,
        elem_scale.reshape(1, SE), elem_stiff, jnp.asarray(own), jnp.asarray(select), jnp.asarray(place),
    )


def solution(mesh):
    flow, shell = ("sec", "dom"), "dom"
    return jax.shard_map(
        on_device,
        mesh=mesh,
        in_specs=(
            P(None, None, flow),
            P(flow),
            P(),
            P(None, flow),
            P(flow),
            P(flow),
            P(None, flow),
            P(None, flow),
            P(flow, None),
            P(flow),
            P(None, shell),
            P(None, shell),
            P(None, shell),
            P(shell),
            P(None, shell),
            P(shell),
            P(),
        ),
        out_specs=(P(None, None, flow), P(None, shell), P(None, flow)),
        check_vma=False,
    )
```

```python
import jax
import jax.numpy as jnp
import numpy as np
from jax import lax
from jax.experimental import pallas as pl
from jax.experimental.pallas import tpu as pltpu
from jax.sharding import PartitionSpec as P

VARS, NP, K, STEPS = 5, 125, 16, 2
E, F, PATCHES, S, SE = 2048, 512, 256, 1024, 1024
HALO, HS, CAP = 256, 32, 128
N_SEC, N_DOM = 8, 16
LIFT, _STEP, SHELL_STEP = 10.0, 0.02, 0.3

TILE = 256
PART = 512
PARTS = (E + 2 * HALO) // PART
ROWS = VARS * 128
SPLIT = 3 * 128
DEPTH = ROWS + 6 * 128
BF, F32, I32 = jnp.bfloat16, jnp.float32, jnp.int32
HIGHEST = lax.Precision.HIGHEST
MESH = pl.DeviceIdType.MESH


def lgl_derivative():
    points = np.array([-1.0, -np.sqrt(3.0 / 7.0), 0.0, np.sqrt(3.0 / 7.0), 1.0])
    barycentric = np.array(
        [
            1.0 / np.prod([points[col] - points[other] for other in range(5) if other != col])
            for col in range(5)
        ]
    )
    derivative = np.zeros((5, 5))
    for row in range(5):
        for col in range(5):
            if row != col:
                derivative[row, col] = (
                    barycentric[col] / barycentric[row] / (points[row] - points[col])
                )
        derivative[row, row] = -np.sum(derivative[row])
    return derivative.astype(np.float32)


def constants():
    nodes = np.arange(NP).reshape(5, 5, 5)
    faces = [nodes[0], nodes[4], nodes[:, 0], nodes[:, 4], nodes[:, :, 0], nodes[:, :, 4]]
    faces = [face.reshape(25) for face in faces]
    d, eye = lgl_derivative(), np.eye(5, dtype=np.float32)
    own = np.zeros((4, 128, 128), np.float32)
    own[0, :NP, :NP] = -np.kron(np.kron(d, eye), eye)
    own[1, :NP, :NP] = -np.kron(np.kron(eye, d), eye)
    own[2, :NP, :NP] = -np.kron(np.kron(eye, eye), d)
    for face in range(6):
        sign = 1.0 if face % 2 else -1.0
        for node in faces[face]:
            own[face // 2, node, node] += sign * 0.5 * LIFT
            own[3, node, node] -= 0.5 * LIFT
    select = np.zeros((VARS, 6 * 32, 128), np.float32)
    place = np.zeros((6, 128, 128), np.float32)
    for face in range(6):
        for n in range(25):
            for w in range(VARS):
                select[w, face * 32 + w + n, faces[face ^ 1][n]] = 1.0
                place[face, faces[face][n], 25 * w + n] = -0.5 * LIFT
    return own, select.astype(jnp.bfloat16), place.astype(jnp.bfloat16)


def dot(a, b):
    return jnp.dot(a, b, preferred_element_type=F32)


def dot_t(a, b):
    return lax.dot_general(a, b, (((1,), (1,)), ((), ())), preferred_element_type=F32)


def halves(x):
    high = x.astype(BF)
    low = (x - high.astype(F32)).astype(BF)
    return jnp.concatenate([high, low], axis=0)


def joined(y):
    rows = y.shape[0] // 2
    return y[:rows] + y[rows:]


def iota(shape, dim):
    return lax.broadcasted_iota(I32, shape, dim)


def one_hot(ids, rows):
    return (iota((rows, ids.shape[1]), 0) == ids).astype(F32)


def kernel(
    state_ref, jac_ref, flux_ref, nb_ref, selem_ref, snode_ref, normal_ref, weight_ref, owner_ref,
    patch_ref, pnode_ref, disp_ref, vel_ref, minv_ref, conn_ref, scale_ref, stiff_ref,
    own_hbm, select_hbm, place_hbm,
    fluid_ref, shell_ref, shift_ref,
    u_ref, own_ref, select_ref, place_ref, x_ref, src_ref, ab_ref, hlo_ref, hhi_ref,
    g_ref, gsend_ref, grecv_ref, ohp_ref, ohn_ref, maskn_ref, ohc_ref, maskc_ref, mask8_ref, ohs_ref,
    wsend_ref, wrecv_ref, wall_ref, tsend_ref, trecv_ref, rsend_ref, rrecv_ref,
    ebuf_ref, erecv_ref, edge_ref, rim_ref, d_ref, v_ref, m_ref,
    local_s, g_s, g_r, flow_s, flow_r, w_s, w_r, t_s, t_r, r_s, r_r, e_s, e_r, rim_s, rim_r,
):
    sec, dom = lax.axis_index("sec"), lax.axis_index("dom")
    line = sec * N_DOM + dom
    devices = N_SEC * N_DOM
    nxt, prv = lax.rem(line + 1, devices), lax.rem(line + devices - 1, devices)
    right = (nxt // N_DOM, lax.rem(nxt, N_DOM))
    left = (prv // N_DOM, lax.rem(prv, N_DOM))

    def dom_peer(d):
        return (sec, lax.rem(dom + d, N_DOM))

    def sec_peer(d):
        return (lax.rem(sec + d, N_SEC), dom)

    def copy(src, dst, send, recv, device):
        return pltpu.make_async_remote_copy(
            src_ref=src, dst_ref=dst, send_sem=send, recv_sem=recv, device_id=device, device_id_type=MESH
        )

    def all_of(src, dst, send, recv):
        return copy(src.at[1 : src.shape[0]], dst.at[1 : dst.shape[0]], send.at[0], recv.at[0], dom_peer(1))

    barrier = pltpu.get_barrier_semaphore()
    greeted = [dom_peer(d) for d in range(1, N_DOM)] + [sec_peer(d) for d in range(1, N_SEC)] + [right, left]
    for device in greeted:
        pl.semaphore_signal(barrier, inc=1, device_id=device, device_id_type=MESH)

    fetch = [
        pltpu.make_async_copy(src, dst, local_s.at[i])
        for i, (src, dst) in enumerate(
            ((state_ref, u_ref), (own_hbm, own_ref), (select_hbm, select_ref), (place_hbm, place_ref))
        )
    ]
    for c in fetch:
        c.start()

    for h in range(8):
        lanes = slice(h * 128, (h + 1) * 128)
        m_ref[h : h + 1, :] = minv_ref[:, lanes]
        for c in range(3):
            d_ref[c * 8 + h : c * 8 + h + 1, :] = disp_ref[c : c + 1, lanes]
            v_ref[c * 8 + h : c * 8 + h + 1, :] = vel_ref[c : c + 1, lanes]

    def edges(step):
        for c in range(3):
            edge_ref[step, 0, c : c + 1, :] = d_ref[c * 8 : c * 8 + 1, :]
            edge_ref[step, 1, c : c + 1, :] = d_ref[c * 8 + 7 : c * 8 + 8, :]

    def rims(step):
        return [
            copy(edge_ref.at[step, 0], rim_ref.at[step, 0], rim_s.at[step, 0], rim_r.at[step, 0], dom_peer(N_DOM - 1)),
            copy(edge_ref.at[step, 1], rim_ref.at[step, 1], rim_s.at[step, 1], rim_r.at[step, 1], dom_peer(1)),
        ]

    edge_ref[...] = jnp.zeros(edge_ref.shape, F32)
    edges(0)

    relative = (owner_ref[...] - dom + N_DOM) & (N_DOM - 1)
    owned = one_hot(relative, N_DOM)
    earlier = (iota((F, F), 0) < iota((F, F), 1)).astype(F32).astype(BF)
    rank = jnp.sum(owned * dot(owned.astype(BF), earlier), axis=0, keepdims=True).astype(I32)
    ohs_ref[...] = one_hot(rank, CAP).astype(BF)

    penalty = None
    for v in range(VARS):
        total = jnp.max(jnp.sum(jnp.abs(flux_ref[v]), axis=1, keepdims=True), axis=0, keepdims=True)
        penalty = total if penalty is None else jnp.maximum(penalty, total)

    def flux(d, v, w):
        return flux_ref[v, d : d + 1, w : w + 1]


    def coupling(face, v, w):
        value = (1.0 if face % 2 else -1.0) * flux(face // 2, v, w)
        return value - penalty if v == w else value

    fetch[0].wait()
    for v in range(VARS):
        x_ref[v * 128 + 112 : v * 128 + 128, :] = jnp.zeros((16, E), BF)
        x_ref[v * 128 : v * 128 + NP, :] = u_ref[v]

    for c in fetch[1:]:
        c.wait()
    choice = select_ref[0].astype(F32) * (-0.5 * LIFT)
    couple = []
    for w in range(VARS):
        blocks = [choice[face * 32 : face * 32 + 32] * coupling(face, VARS - 1, w) for face in range(6)]
        couple.append(jnp.concatenate(blocks, axis=0).astype(BF))
    couple = jnp.concatenate(couple, axis=1)
    gsend_ref[0] = dot(couple, x_ref[0:ROWS, E - HALO : E]).astype(BF)
    gsend_ref[1] = dot(couple, x_ref[0:ROWS, 0:HALO]).astype(BF)

    pl.semaphore_wait(barrier, len(greeted))
    first = [
        copy(gsend_ref.at[0], grecv_ref.at[0], g_s.at[0], g_r.at[0], right),
        copy(gsend_ref.at[1], grecv_ref.at[1], g_s.at[1], g_r.at[1], left),
    ]
    for c in first:
        c.start()
    rim0 = rims(0)
    for c in rim0:
        c.start()
    flow = [
        (
            copy(x_ref.at[rows, E - HALO : E], hlo_ref.at[rows], flow_s.at[0, lot], flow_r.at[0, lot], right),
            copy(x_ref.at[rows, 0:HALO], hhi_ref.at[rows], flow_s.at[1, lot], flow_r.at[1, lot], left),
        )
        for lot, rows in enumerate((slice(0, SPLIT), slice(SPLIT, ROWS)))
    ]
    for c in flow[0]:
        c.start()

    def spread_faces(values, part):
        for face in range(6):
            g_ref[face, part * 32 : part * 32 + 32, :] = values[face * 32 : face * 32 + 32]

    def operator(v):
        for w in range(VARS):
            block = flux(0, v, w) * own_ref[0] + flux(1, v, w) * own_ref[1] + flux(2, v, w) * own_ref[2]
            if v == w:
                block = block + penalty * own_ref[3]
            ab_ref[v * 128 : v * 128 + 128, w * 128 : w * 128 + 128] = block.astype(BF)

    operator(VARS - 1)

    last = slice((VARS - 1) * 128, VARS * 128)
    elems = selem_ref[...]
    picker = one_hot(elems & (TILE - 1), TILE).astype(BF)
    base, near = jnp.zeros((128, F), F32), jnp.zeros((16, F), F32)
    for h in range(E // TILE):
        cols = slice(h * TILE, (h + 1) * TILE)
        factor = _STEP * jac_ref[:, cols]
        spread_faces(dot(couple, x_ref[0:ROWS, cols]).astype(BF), h + 1)
        moved = x_ref[last, cols].astype(F32) + factor * dot(ab_ref[last, 0:ROWS], x_ref[0:ROWS, cols])
        ids = nb_ref[:, cols]
        rows = jnp.concatenate(
            [halves(factor), (ids & 255).astype(F32).astype(BF), (ids >> 8).astype(F32).astype(BF)], axis=0
        )
        rows = jnp.concatenate([halves(moved), rows, jnp.zeros((2, TILE), BF)], axis=0)
        found = dot(rows, picker)
        mine = (elems // TILE) == h
        base = jnp.where(mine, joined(found[0:256]), base)
        near = jnp.where(mine, found[256:272], near)
    surf_factor = near[0:1] + near[1:2]
    column_of, block_of = near[2:8].astype(I32), near[8:14].astype(I32)

    payload = jnp.concatenate([weight_ref[...], patch_ref[...].astype(F32), jnp.zeros((15, F), F32)], axis=0)
    payload = jnp.concatenate([payload * owned[d : d + 1] for d in range(N_DOM)], axis=0)
    placed = dot_t(payload.astype(BF), ohs_ref[...])
    wsend_ref[...] = placed.astype(BF).reshape(N_DOM, 32, CAP)

    early = [copy(wsend_ref.at[d], wrecv_ref.at[d], w_s.at[0], w_r.at[0], dom_peer(d)) for d in range(1, N_DOM)]
    for c in early:
        c.start()
    wrecv_ref[0] = wsend_ref[0]

    for k in range(K):
        ids = pnode_ref[k : k + 1, :]
        lanes = slice(k * PATCHES, (k + 1) * PATCHES)
        ohn_ref[:, lanes] = one_hot(ids & 127, 128).astype(BF)
        maskn_ref[:, lanes] = one_hot(ids >> 7, 8)
    for v in range(VARS - 1):
        operator(v)
    column = iota((1, 128), 1)
    for face in range(6):
        where = place_ref[face].astype(F32)
        for v in range(VARS):
            factor = jnp.zeros((1, 128), F32)
            for w in range(VARS):
                factor = jnp.where((column >= 25 * w) & (column < 25 * w + 25), coupling(face, v, w), factor)
            ab_ref[v * 128 : v * 128 + 128, ROWS + face * 128 : ROWS + face * 128 + 128] = (where * factor).astype(BF)

    for c in first:
        c.wait()
    keep_hi = jnp.where(line < devices - 1, 1.0, 0.0).astype(BF)
    keep_lo = jnp.where(line > 0, 1.0, 0.0).astype(BF)
    spread_faces(grecv_ref[0] * keep_lo, 0)
    spread_faces(grecv_ref[1] * keep_hi, E // HALO + 1)
    n = iota((32, F), 0)
    i, j = (n * 13) >> 6, n - 5 * ((n * 13) >> 6)
    added = jnp.zeros((32, F), F32)
    for face in range(6):
        picked = dot(g_ref[face], one_hot(column_of[face : face + 1], HALO).astype(BF))
        block = block_of[face : face + 1]
        other = picked[0:32]
        for p in range(1, E // HALO + 2):
            other = jnp.where(block == p, picked[p * 32 : p * 32 + 32], other)
        node = (n, n + 100, 25 * i + j, 25 * i + j + 20, 5 * n, 5 * n + 4)[face]
        added = added + jnp.where((node == snode_ref[...]) & (n < 25), other, 0.0)
    own_part = jnp.sum(jnp.where(iota((128, F), 0) == snode_ref[...], base, 0.0), axis=0, keepdims=True)
    pressure = own_part + surf_factor * jnp.sum(added, axis=0, keepdims=True)
    pressure = pressure.astype(BF).astype(F32)
    traction = jnp.concatenate([normal_ref[...] * pressure, jnp.zeros((5, F), F32)], axis=0)
    rows = jnp.concatenate([traction * owned[d : d + 1] for d in range(N_DOM)], axis=0)
    tsend_ref[...] = joined(dot_t(halves(rows), ohs_ref[...])).reshape(N_DOM, 8, CAP)
    loads = [copy(tsend_ref.at[d], trecv_ref.at[d], t_s.at[0], t_r.at[0], dom_peer(d)) for d in range(1, N_DOM)]
    for c in loads:
        c.start()
    for c in flow[1]:
        c.start()
    trecv_ref[0] = tsend_ref[0]

    def neighbour(face, ids):
        ids = jnp.where(ids >= HALO, ids - HALO, ids + (E + HALO))
        picked = dot(src_ref[face], one_hot(ids & (PART - 1), PART).astype(BF))
        part = ids // PART
        other = picked[0:128]
        for p in range(1, PARTS):
            other = jnp.where(part == p, picked[p * 128 : p * 128 + 128], other)
        return other.astype(BF)

    def advance(t, carry):
        cols = pl.ds(pl.multiple_of(t * TILE, TILE), TILE)
        for face in range(6):
            x_ref[ROWS + face * 128 : ROWS + face * 128 + 128, cols] = neighbour(face, nb_ref[face : face + 1, cols])
        factor = _STEP * jac_ref[:, cols]
        change = dot(ab_ref[...], x_ref[:, cols])
        for v in range(VARS):
            moved = x_ref[v * 128 : v * 128 + 128, cols].astype(F32) + factor * change[v * 128 : v * 128 + 128]
            fluid_ref[v, :, cols] = moved.astype(BF)[:NP]
        return carry

    tiles = (0, 3, 2, 3)

    def fill(wait):
        lax.fori_loop(sum(tiles[:wait]), sum(tiles[: wait + 1]), advance, 0, unroll=True)

    def extract(values, part, lanes):
        e = [dot(select_ref[w], values(w)) for w in range(VARS)]
        for face in range(6):
            g = [x[face * 32 : face * 32 + 32] for x in e]
            pieces = [g[0][0:24]]
            for w in range(1, VARS):
                pieces += [g[w - 1][24:32] + g[w][0:8], g[w][8:24]]
            pieces += [g[VARS - 1][24:32]]
            src_ref[face, pl.ds(part * 128, 128), lanes] = jnp.concatenate(pieces, axis=0).astype(BF)

    for part in range(E // PART):
        for half in range(PART // TILE):
            cols = slice(part * PART + half * TILE, part * PART + (half + 1) * TILE)
            extract(lambda w: x_ref[w * 128 : w * 128 + 128, cols], part, slice(half * TILE, (half + 1) * TILE))

    def internal(step):
        lane = iota((8, 128), 1)
        from_right = rim_ref[step, 0] * jnp.where(dom < N_DOM - 1, 1.0, 0.0)
        from_left = rim_ref[step, 1] * jnp.where(dom > 0, 1.0, 0.0)
        rim = jnp.where(lane < 64, from_right, from_left)
        read = joined(dot(halves(jnp.concatenate([d_ref[...], rim], axis=0)), ohc_ref[...]))
        picked = []
        for c in range(3):
            values = jnp.sum(read[c * 8 : c * 8 + 8] * maskc_ref[...], axis=0, keepdims=True)
            values = values + read[24 + c : 25 + c] * mask8_ref[...]
            picked += [values[:, q * SE : (q + 1) * SE] for q in range(4)]
        force = jnp.dot(
            stiff_ref[...], jnp.concatenate(picked, axis=0), precision=HIGHEST, preferred_element_type=F32
        )
        force = force * scale_ref[...]
        spread = []
        for c in range(3):
            line_c = jnp.concatenate([force[c * 4 + q : c * 4 + q + 1] for q in range(4)], axis=1)
            spread.append(line_c * maskc_ref[...])
        return joined(dot_t(halves(jnp.concatenate(spread, axis=0)), ohc_ref[...]))

    for q in range(4):
        ids = conn_ref[q : q + 1, :]
        ids = jnp.where(ids >= HS, ids - HS, ids + (S + 128 - HS))
        lanes = slice(q * SE, (q + 1) * SE)
        ohc_ref[:, lanes] = one_hot(ids & 127, 128).astype(BF)
        maskc_ref[:, lanes] = one_hot(ids >> 7, 8)
        mask8_ref[:, lanes] = ((ids >> 7) == 8).astype(F32)

    for c in rim0:
        c.wait()
    inner = internal(0)

    all_of(wsend_ref, wrecv_ref, w_s, w_r).wait()
    for d in range(N_DOM):
        block = wrecv_ref[d].astype(F32)
        wall_ref[:, d * CAP : (d + 1) * CAP] = block[0:K]
        ohp_ref[:, d * CAP : (d + 1) * CAP] = one_hot(block[K : K + 1].astype(I32), PATCHES).astype(BF)
    fill(0)

    all_of(tsend_ref, trecv_ref, t_s, t_r).wait()
    load = []
    for c in range(3):
        line_c = jnp.concatenate([trecv_ref[d, c : c + 1, :] for d in range(N_DOM)], axis=1)
        load.append(wall_ref[...] * line_c)
    by_patch = joined(dot_t(halves(jnp.concatenate(load, axis=0)), ohp_ref[...]))
    spread = []
    for c in range(3):
        line_c = jnp.concatenate([by_patch[c * K + k : c * K + k + 1] for k in range(K)], axis=1)
        spread.append(line_c * maskn_ref[...])
    partial = joined(dot_t(halves(jnp.concatenate(spread, axis=0)), ohn_ref[...]))
    ebuf_ref[...] = partial
    sums = [copy(ebuf_ref, erecv_ref.at[d], e_s.at[0], e_r.at[0], sec_peer(d)) for d in range(1, N_SEC)]
    for c in sums:
        c.start()
    erecv_ref[0] = partial

    for lot in flow:
        for c in lot:
            c.wait()
    extract(lambda w: hhi_ref[w * 128 : w * 128 + 128, :] * keep_hi, PARTS - 1, slice(0, HALO))
    extract(lambda w: hlo_ref[w * 128 : w * 128 + 128, :] * keep_lo, PARTS - 1, slice(HALO, 2 * HALO))
    fill(1)
    all_of(erecv_ref, erecv_ref, e_s, e_r).wait()
    external = erecv_ref[lax.rem(sec, N_SEC)]
    for s in range(1, N_SEC):
        external = external + erecv_ref[lax.rem(sec - s + N_SEC, N_SEC)]

    mass = jnp.concatenate([m_ref[...]] * 3, axis=0)
    for step in range(STEPS):
        if step > 0:
            edges(step)
            around = rims(step)
            for c in around:
                c.start()
            fill(2)
            for c in around:
                c.wait()
            inner = internal(step)
        velocity = v_ref[...] + SHELL_STEP * mass * (external - inner)
        v_ref[...] = velocity
        d_ref[...] = d_ref[...] + SHELL_STEP * velocity

    read = joined(dot(halves(d_ref[...]), ohn_ref[...]))
    nodes = []
    for c in range(3):
        values = jnp.sum(read[c * 8 : c * 8 + 8] * maskn_ref[...], axis=0, keepdims=True)
        nodes += [values[:, k * PATCHES : (k + 1) * PATCHES] for k in range(K)]
    by_row = joined(dot(halves(jnp.concatenate(nodes, axis=0)), ohp_ref[...]))
    rsend_ref[...] = jnp.zeros(rsend_ref.shape, F32)
    for c in range(3):
        total = jnp.sum(by_row[c * K : (c + 1) * K] * wall_ref[...], axis=0, keepdims=True)
        for d in range(N_DOM):
            rsend_ref[d, c : c + 1, :] = total[:, d * CAP : (d + 1) * CAP]
    returns = [
        copy(rsend_ref.at[d], rrecv_ref.at[d], r_s.at[0], r_r.at[0], dom_peer(N_DOM - d)) for d in range(1, N_DOM)
    ]
    for c in returns:
        c.start()
    rrecv_ref[0] = rsend_ref[0]
    for h in range(8):
        for c in range(3):
            shell_ref[c : c + 1, h * 128 : (h + 1) * 128] = d_ref[c * 8 + h : c * 8 + h + 1, :]
    fill(3)
    all_of(rsend_ref, rrecv_ref, r_s, r_r).wait()
    back = joined(dot(halves(rrecv_ref[...].reshape(N_DOM * 8, CAP)), ohs_ref[...]))
    shift = back[0:8] * owned[0:1]
    for d in range(1, N_DOM):
        shift = shift + back[d * 8 : d * 8 + 8] * owned[d : d + 1]
    shift_ref[...] = shift[0:3]


def on_device(
    fluid_state, jac_inv, flux_mats, neighbours, surf_elem, surf_node, normals, rbf_weights, owners,
    patches, patch_nodes, shell_disp, shell_vel, mass_inv, shell_conn, elem_scale, elem_stiff,
):
    own, select, place = constants()
    vmem, hbm = pl.BlockSpec(memory_space=pltpu.VMEM), pl.BlockSpec(memory_space=pl.ANY)
    dma = pltpu.SemaphoreType.DMA
    return pl.pallas_call(
        kernel,
        out_shape=(
            pltpu.VMEM((VARS, NP, E), BF),
            pltpu.VMEM((3, S), F32),
            pltpu.VMEM((3, F), F32),
        ),
        in_specs=[hbm] + [vmem] * 16 + [hbm] * 3,
        out_specs=(vmem, vmem, vmem),
        scratch_shapes=[
            pltpu.VMEM((VARS, NP, E), BF),
            pltpu.VMEM((4, 128, 128), F32),
            pltpu.VMEM((VARS, 6 * 32, 128), BF),
            pltpu.VMEM((6, 128, 128), BF),
            pltpu.VMEM((DEPTH, E), BF),
            pltpu.VMEM((6, PARTS * 128, PART), BF),
            pltpu.VMEM((ROWS, DEPTH), BF),
            pltpu.VMEM((ROWS, HALO), BF),
            pltpu.VMEM((ROWS, HALO), BF),
            pltpu.VMEM((6, (E // HALO + 2) * 32, HALO), BF),
            pltpu.VMEM((2, 6 * 32, HALO), BF),
            pltpu.VMEM((2, 6 * 32, HALO), BF),
            pltpu.VMEM((PATCHES, N_DOM * CAP), BF),
            pltpu.VMEM((128, K * PATCHES), BF),
            pltpu.VMEM((8, K * PATCHES), F32),
            pltpu.VMEM((128, 4 * SE), BF),
            pltpu.VMEM((8, 4 * SE), F32),
            pltpu.VMEM((1, 4 * SE), F32),
            pltpu.VMEM((CAP, F), BF),
            pltpu.VMEM((N_DOM, 32, CAP), BF),
            pltpu.VMEM((N_DOM, 32, CAP), BF),
            pltpu.VMEM((K, N_DOM * CAP), F32),
            pltpu.VMEM((N_DOM, 8, CAP), F32),
            pltpu.VMEM((N_DOM, 8, CAP), F32),
            pltpu.VMEM((N_DOM, 8, CAP), F32),
            pltpu.VMEM((N_DOM, 8, CAP), F32),
            pltpu.VMEM((24, 128), F32),
            pltpu.VMEM((N_SEC, 24, 128), F32),
            pltpu.VMEM((STEPS, 2, 8, 128), F32),
            pltpu.VMEM((STEPS, 2, 8, 128), F32),
            pltpu.VMEM((24, 128), F32),
            pltpu.VMEM((24, 128), F32),
            pltpu.VMEM((8, 128), F32),
            dma((4,)), dma((2,)), dma((2,)), dma((2, 2)), dma((2, 2)),
            dma((1,)), dma((1,)),
            dma((1,)), dma((1,)),
            dma((1,)), dma((1,)),
            dma((1,)), dma((1,)),
            dma((STEPS, 2)), dma((STEPS, 2)),
        ],
        compiler_params=pltpu.CompilerParams(
            collective_id=0, has_side_effects=True, vmem_limit_bytes=56 * 1024 * 1024
        ),
    )(
        fluid_state, jac_inv.reshape(1, E), jnp.transpose(flux_mats, (1, 0, 2)), neighbours, surf_elem.reshape(1, F),
        surf_node.reshape(1, F), normals, rbf_weights, owners.reshape(1, F), patches.reshape(1, F),
        patch_nodes, shell_disp, shell_vel, mass_inv.reshape(1, S), shell_conn,
        elem_scale.reshape(1, SE), elem_stiff, jnp.asarray(own), jnp.asarray(select), jnp.asarray(place),
    )


def solution(mesh):
    flow, shell = ("sec", "dom"), "dom"
    return jax.shard_map(
        on_device,
        mesh=mesh,
        in_specs=(
            P(None, None, flow),
            P(flow),
            P(),
            P(None, flow),
            P(flow),
            P(flow),
            P(None, flow),
            P(None, flow),
            P(flow, None),
            P(flow),
            P(None, shell),
            P(None, shell),
            P(None, shell),
            P(shell),
            P(None, shell),
            P(shell),
            P(),
        ),
        out_specs=(P(None, None, flow), P(None, shell), P(None, flow)),
        check_vma=False,
    )
```

```python
import jax
import jax.numpy as jnp
import numpy as np
from jax import lax
from jax.experimental import pallas as pl
from jax.experimental.pallas import tpu as pltpu
from jax.sharding import PartitionSpec as P

VARS, NP, K, STEPS = 5, 125, 16, 2
E, F, PATCHES, S, SE = 2048, 512, 256, 1024, 1024
HALO, HS, CAP = 256, 32, 128
N_SEC, N_DOM = 8, 16
LIFT, _STEP, SHELL_STEP = 10.0, 0.02, 0.3

TILE = 256
PART = 512
PARTS = (E + 2 * HALO) // PART
ROWS = VARS * 128
SPLIT = 4 * 128
DEPTH = ROWS + 6 * 128
BF, F32, I32 = jnp.bfloat16, jnp.float32, jnp.int32
HIGHEST = lax.Precision.HIGHEST
MESH = pl.DeviceIdType.MESH


def lgl_derivative():
    points = np.array([-1.0, -np.sqrt(3.0 / 7.0), 0.0, np.sqrt(3.0 / 7.0), 1.0])
    barycentric = np.array(
        [
            1.0 / np.prod([points[col] - points[other] for other in range(5) if other != col])
            for col in range(5)
        ]
    )
    derivative = np.zeros((5, 5))
    for row in range(5):
        for col in range(5):
            if row != col:
                derivative[row, col] = (
                    barycentric[col] / barycentric[row] / (points[row] - points[col])
                )
        derivative[row, row] = -np.sum(derivative[row])
    return derivative.astype(np.float32)


def constants():
    nodes = np.arange(NP).reshape(5, 5, 5)
    faces = [nodes[0], nodes[4], nodes[:, 0], nodes[:, 4], nodes[:, :, 0], nodes[:, :, 4]]
    faces = [face.reshape(25) for face in faces]
    d, eye = lgl_derivative(), np.eye(5, dtype=np.float32)
    own = np.zeros((4, 128, 128), np.float32)
    own[0, :NP, :NP] = -np.kron(np.kron(d, eye), eye)
    own[1, :NP, :NP] = -np.kron(np.kron(eye, d), eye)
    own[2, :NP, :NP] = -np.kron(np.kron(eye, eye), d)
    for face in range(6):
        sign = 1.0 if face % 2 else -1.0
        for node in faces[face]:
            own[face // 2, node, node] += sign * 0.5 * LIFT
            own[3, node, node] -= 0.5 * LIFT
    select = np.zeros((VARS, 6 * 32, 128), np.float32)
    place = np.zeros((6, 128, 128), np.float32)
    for face in range(6):
        for n in range(25):
            for w in range(VARS):
                select[w, face * 32 + w + n, faces[face ^ 1][n]] = 1.0
                place[face, faces[face][n], 25 * w + n] = -0.5 * LIFT
    return own, select.astype(jnp.bfloat16), place.astype(jnp.bfloat16)


def dot(a, b):
    return jnp.dot(a, b, preferred_element_type=F32)


def dot_t(a, b):
    return lax.dot_general(a, b, (((1,), (1,)), ((), ())), preferred_element_type=F32)


def halves(x):
    high = x.astype(BF)
    low = (x - high.astype(F32)).astype(BF)
    return jnp.concatenate([high, low], axis=0)


def joined(y):
    rows = y.shape[0] // 2
    return y[:rows] + y[rows:]


def iota(shape, dim):
    return lax.broadcasted_iota(I32, shape, dim)


def one_hot(ids, rows):
    return (iota((rows, ids.shape[1]), 0) == ids).astype(F32)


def kernel(
    state_ref, jac_ref, flux_ref, nb_ref, selem_ref, snode_ref, normal_ref, weight_ref, owner_ref,
    patch_ref, pnode_ref, disp_ref, vel_ref, minv_ref, conn_ref, scale_ref, stiff_ref,
    own_hbm, select_hbm, place_hbm,
    fluid_ref, shell_ref, shift_ref,
    u_ref, own_ref, select_ref, place_ref, x_ref, src_ref, ab_ref, hlo_ref, hhi_ref,
    g_ref, gsend_ref, grecv_ref, ohp_ref, ohn_ref, maskn_ref, ohc_ref, maskc_ref, mask8_ref, ohs_ref,
    wsend_ref, wrecv_ref, wall_ref, tsend_ref, trecv_ref, rsend_ref, rrecv_ref,
    ebuf_ref, erecv_ref, edge_ref, rim_ref, d_ref, v_ref, m_ref,
    local_s, g_s, g_r, flow_s, flow_r, w_s, w_r, t_s, t_r, r_s, r_r, e_s, e_r, rim_s, rim_r,
):
    sec, dom = lax.axis_index("sec"), lax.axis_index("dom")
    line = sec * N_DOM + dom
    devices = N_SEC * N_DOM
    nxt, prv = lax.rem(line + 1, devices), lax.rem(line + devices - 1, devices)
    right = (nxt // N_DOM, lax.rem(nxt, N_DOM))
    left = (prv // N_DOM, lax.rem(prv, N_DOM))

    def dom_peer(d):
        return (sec, lax.rem(dom + d, N_DOM))

    def sec_peer(d):
        return (lax.rem(sec + d, N_SEC), dom)

    def copy(src, dst, send, recv, device):
        return pltpu.make_async_remote_copy(
            src_ref=src, dst_ref=dst, send_sem=send, recv_sem=recv, device_id=device, device_id_type=MESH
        )

    def all_of(src, dst, send, recv):
        return copy(src.at[1 : src.shape[0]], dst.at[1 : dst.shape[0]], send.at[0], recv.at[0], dom_peer(1))

    barrier = pltpu.get_barrier_semaphore()
    greeted = [dom_peer(d) for d in range(1, N_DOM)] + [sec_peer(d) for d in range(1, N_SEC)] + [right, left]
    for device in greeted:
        pl.semaphore_signal(barrier, inc=1, device_id=device, device_id_type=MESH)

    fetch = [
        pltpu.make_async_copy(src, dst, local_s.at[i])
        for i, (src, dst) in enumerate(
            ((state_ref, u_ref), (own_hbm, own_ref), (select_hbm, select_ref), (place_hbm, place_ref))
        )
    ]
    for c in fetch:
        c.start()

    for h in range(8):
        lanes = slice(h * 128, (h + 1) * 128)
        m_ref[h : h + 1, :] = minv_ref[:, lanes]
        for c in range(3):
            d_ref[c * 8 + h : c * 8 + h + 1, :] = disp_ref[c : c + 1, lanes]
            v_ref[c * 8 + h : c * 8 + h + 1, :] = vel_ref[c : c + 1, lanes]

    def edges(step):
        for c in range(3):
            edge_ref[step, 0, c : c + 1, :] = d_ref[c * 8 : c * 8 + 1, :]
            edge_ref[step, 1, c : c + 1, :] = d_ref[c * 8 + 7 : c * 8 + 8, :]

    def rims(step):
        return [
            copy(edge_ref.at[step, 0], rim_ref.at[step, 0], rim_s.at[step, 0], rim_r.at[step, 0], dom_peer(N_DOM - 1)),
            copy(edge_ref.at[step, 1], rim_ref.at[step, 1], rim_s.at[step, 1], rim_r.at[step, 1], dom_peer(1)),
        ]

    edge_ref[...] = jnp.zeros(edge_ref.shape, F32)
    edges(0)

    relative = (owner_ref[...] - dom + N_DOM) & (N_DOM - 1)
    owned = one_hot(relative, N_DOM)
    earlier = (iota((F, F), 0) < iota((F, F), 1)).astype(F32).astype(BF)
    rank = jnp.sum(owned * dot(owned.astype(BF), earlier), axis=0, keepdims=True).astype(I32)
    ohs_ref[...] = one_hot(rank, CAP).astype(BF)

    penalty = None
    for v in range(VARS):
        total = jnp.max(jnp.sum(jnp.abs(flux_ref[v]), axis=1, keepdims=True), axis=0, keepdims=True)
        penalty = total if penalty is None else jnp.maximum(penalty, total)

    def flux(d, v, w):
        return flux_ref[v, d : d + 1, w : w + 1]


    def coupling(face, v, w):
        value = (1.0 if face % 2 else -1.0) * flux(face // 2, v, w)
        return value - penalty if v == w else value

    fetch[0].wait()
    for v in range(VARS):
        x_ref[v * 128 + 112 : v * 128 + 128, :] = jnp.zeros((16, E), BF)
        x_ref[v * 128 : v * 128 + NP, :] = u_ref[v]

    for c in fetch[1:]:
        c.wait()
    choice = select_ref[0].astype(F32) * (-0.5 * LIFT)
    couple = []
    for w in range(VARS):
        blocks = [choice[face * 32 : face * 32 + 32] * coupling(face, VARS - 1, w) for face in range(6)]
        couple.append(jnp.concatenate(blocks, axis=0).astype(BF))
    couple = jnp.concatenate(couple, axis=1)
    gsend_ref[0] = dot(couple, x_ref[0:ROWS, E - HALO : E]).astype(BF)
    gsend_ref[1] = dot(couple, x_ref[0:ROWS, 0:HALO]).astype(BF)

    pl.semaphore_wait(barrier, len(greeted))
    first = [
        copy(gsend_ref.at[0], grecv_ref.at[0], g_s.at[0], g_r.at[0], right),
        copy(gsend_ref.at[1], grecv_ref.at[1], g_s.at[1], g_r.at[1], left),
    ]
    for c in first:
        c.start()
    rim0 = rims(0)
    for c in rim0:
        c.start()
    flow = [
        (
            copy(x_ref.at[rows, E - HALO : E], hlo_ref.at[rows], flow_s.at[0, lot], flow_r.at[0, lot], right),
            copy(x_ref.at[rows, 0:HALO], hhi_ref.at[rows], flow_s.at[1, lot], flow_r.at[1, lot], left),
        )
        for lot, rows in enumerate((slice(0, SPLIT), slice(SPLIT, ROWS)))
    ]
    for c in flow[0]:
        c.start()

    def spread_faces(values, part):
        for face in range(6):
            g_ref[face, part * 32 : part * 32 + 32, :] = values[face * 32 : face * 32 + 32]

    def operator(v):
        for w in range(VARS):
            block = flux(0, v, w) * own_ref[0] + flux(1, v, w) * own_ref[1] + flux(2, v, w) * own_ref[2]
            if v == w:
                block = block + penalty * own_ref[3]
            ab_ref[v * 128 : v * 128 + 128, w * 128 : w * 128 + 128] = block.astype(BF)

    operator(VARS - 1)

    last = slice((VARS - 1) * 128, VARS * 128)
    elems = selem_ref[...]
    picker = one_hot(elems & (TILE - 1), TILE).astype(BF)
    base, near = jnp.zeros((128, F), F32), jnp.zeros((16, F), F32)
    for h in range(E // TILE):
        cols = slice(h * TILE, (h + 1) * TILE)
        factor = _STEP * jac_ref[:, cols]
        spread_faces(dot(couple, x_ref[0:ROWS, cols]).astype(BF), h + 1)
        moved = x_ref[last, cols].astype(F32) + factor * dot(ab_ref[last, 0:ROWS], x_ref[0:ROWS, cols])
        ids = nb_ref[:, cols]
        rows = jnp.concatenate(
            [halves(factor), (ids & 255).astype(F32).astype(BF), (ids >> 8).astype(F32).astype(BF)], axis=0
        )
        rows = jnp.concatenate([halves(moved), rows, jnp.zeros((2, TILE), BF)], axis=0)
        found = dot(rows, picker)
        mine = (elems // TILE) == h
        base = jnp.where(mine, joined(found[0:256]), base)
        near = jnp.where(mine, found[256:272], near)
    surf_factor = near[0:1] + near[1:2]
    column_of, block_of = near[2:8].astype(I32), near[8:14].astype(I32)

    payload = jnp.concatenate([weight_ref[...], patch_ref[...].astype(F32), jnp.zeros((15, F), F32)], axis=0)
    payload = jnp.concatenate([payload * owned[d : d + 1] for d in range(N_DOM)], axis=0)
    placed = dot_t(payload.astype(BF), ohs_ref[...])
    wsend_ref[...] = placed.astype(BF).reshape(N_DOM, 32, CAP)

    early = [copy(wsend_ref.at[d], wrecv_ref.at[d], w_s.at[0], w_r.at[0], dom_peer(d)) for d in range(1, N_DOM)]
    for c in early:
        c.start()
    wrecv_ref[0] = wsend_ref[0]

    for k in range(K):
        ids = pnode_ref[k : k + 1, :]
        lanes = slice(k * PATCHES, (k + 1) * PATCHES)
        ohn_ref[:, lanes] = one_hot(ids & 127, 128).astype(BF)
        maskn_ref[:, lanes] = one_hot(ids >> 7, 8)
    for v in range(VARS - 1):
        operator(v)
    column = iota((1, 128), 1)
    for face in range(6):
        where = place_ref[face].astype(F32)
        for v in range(VARS):
            factor = jnp.zeros((1, 128), F32)
            for w in range(VARS):
                factor = jnp.where((column >= 25 * w) & (column < 25 * w + 25), coupling(face, v, w), factor)
            ab_ref[v * 128 : v * 128 + 128, ROWS + face * 128 : ROWS + face * 128 + 128] = (where * factor).astype(BF)

    for c in first:
        c.wait()
    keep_hi = jnp.where(line < devices - 1, 1.0, 0.0).astype(BF)
    keep_lo = jnp.where(line > 0, 1.0, 0.0).astype(BF)
    spread_faces(grecv_ref[0] * keep_lo, 0)
    spread_faces(grecv_ref[1] * keep_hi, E // HALO + 1)
    n = iota((32, F), 0)
    i, j = (n * 13) >> 6, n - 5 * ((n * 13) >> 6)
    added = jnp.zeros((32, F), F32)
    for face in range(6):
        picked = dot(g_ref[face], one_hot(column_of[face : face + 1], HALO).astype(BF))
        block = block_of[face : face + 1]
        other = picked[0:32]
        for p in range(1, E // HALO + 2):
            other = jnp.where(block == p, picked[p * 32 : p * 32 + 32], other)
        node = (n, n + 100, 25 * i + j, 25 * i + j + 20, 5 * n, 5 * n + 4)[face]
        added = added + jnp.where((node == snode_ref[...]) & (n < 25), other, 0.0)
    own_part = jnp.sum(jnp.where(iota((128, F), 0) == snode_ref[...], base, 0.0), axis=0, keepdims=True)
    pressure = own_part + surf_factor * jnp.sum(added, axis=0, keepdims=True)
    pressure = pressure.astype(BF).astype(F32)
    traction = jnp.concatenate([normal_ref[...] * pressure, jnp.zeros((5, F), F32)], axis=0)
    rows = jnp.concatenate([traction * owned[d : d + 1] for d in range(N_DOM)], axis=0)
    tsend_ref[...] = joined(dot_t(halves(rows), ohs_ref[...])).reshape(N_DOM, 8, CAP)
    loads = [copy(tsend_ref.at[d], trecv_ref.at[d], t_s.at[0], t_r.at[0], dom_peer(d)) for d in range(1, N_DOM)]
    for c in loads:
        c.start()
    for c in flow[1]:
        c.start()
    trecv_ref[0] = tsend_ref[0]

    def neighbour(face, ids):
        ids = jnp.where(ids >= HALO, ids - HALO, ids + (E + HALO))
        picked = dot(src_ref[face], one_hot(ids & (PART - 1), PART).astype(BF))
        part = ids // PART
        other = picked[0:128]
        for p in range(1, PARTS):
            other = jnp.where(part == p, picked[p * 128 : p * 128 + 128], other)
        return other.astype(BF)

    def advance(t, carry):
        cols = pl.ds(pl.multiple_of(t * TILE, TILE), TILE)
        for face in range(6):
            x_ref[ROWS + face * 128 : ROWS + face * 128 + 128, cols] = neighbour(face, nb_ref[face : face + 1, cols])
        factor = _STEP * jac_ref[:, cols]
        change = dot(ab_ref[...], x_ref[:, cols])
        for v in range(VARS):
            moved = x_ref[v * 128 : v * 128 + 128, cols].astype(F32) + factor * change[v * 128 : v * 128 + 128]
            fluid_ref[v, :, cols] = moved.astype(BF)[:NP]
        return carry

    tiles = (0, 3, 2, 3)

    def fill(wait):
        lax.fori_loop(sum(tiles[:wait]), sum(tiles[: wait + 1]), advance, 0, unroll=True)

    def extract(values, part, lanes):
        e = [dot(select_ref[w], values(w)) for w in range(VARS)]
        for face in range(6):
            g = [x[face * 32 : face * 32 + 32] for x in e]
            pieces = [g[0][0:24]]
            for w in range(1, VARS):
                pieces += [g[w - 1][24:32] + g[w][0:8], g[w][8:24]]
            pieces += [g[VARS - 1][24:32]]
            src_ref[face, pl.ds(part * 128, 128), lanes] = jnp.concatenate(pieces, axis=0).astype(BF)

    for part in range(E // PART):
        for half in range(PART // TILE):
            cols = slice(part * PART + half * TILE, part * PART + (half + 1) * TILE)
            extract(lambda w: x_ref[w * 128 : w * 128 + 128, cols], part, slice(half * TILE, (half + 1) * TILE))

    def internal(step):
        lane = iota((8, 128), 1)
        from_right = rim_ref[step, 0] * jnp.where(dom < N_DOM - 1, 1.0, 0.0)
        from_left = rim_ref[step, 1] * jnp.where(dom > 0, 1.0, 0.0)
        rim = jnp.where(lane < 64, from_right, from_left)
        read = joined(dot(halves(jnp.concatenate([d_ref[...], rim], axis=0)), ohc_ref[...]))
        picked = []
        for c in range(3):
            values = jnp.sum(read[c * 8 : c * 8 + 8] * maskc_ref[...], axis=0, keepdims=True)
            values = values + read[24 + c : 25 + c] * mask8_ref[...]
            picked += [values[:, q * SE : (q + 1) * SE] for q in range(4)]
        force = jnp.dot(
            stiff_ref[...], jnp.concatenate(picked, axis=0), precision=HIGHEST, preferred_element_type=F32
        )
        force = force * scale_ref[...]
        spread = []
        for c in range(3):
            line_c = jnp.concatenate([force[c * 4 + q : c * 4 + q + 1] for q in range(4)], axis=1)
            spread.append(line_c * maskc_ref[...])
        return joined(dot_t(halves(jnp.concatenate(spread, axis=0)), ohc_ref[...]))

    for q in range(4):
        ids = conn_ref[q : q + 1, :]
        ids = jnp.where(ids >= HS, ids - HS, ids + (S + 128 - HS))
        lanes = slice(q * SE, (q + 1) * SE)
        ohc_ref[:, lanes] = one_hot(ids & 127, 128).astype(BF)
        maskc_ref[:, lanes] = one_hot(ids >> 7, 8)
        mask8_ref[:, lanes] = ((ids >> 7) == 8).astype(F32)

    for c in rim0:
        c.wait()
    inner = internal(0)

    all_of(wsend_ref, wrecv_ref, w_s, w_r).wait()
    for d in range(N_DOM):
        block = wrecv_ref[d].astype(F32)
        wall_ref[:, d * CAP : (d + 1) * CAP] = block[0:K]
        ohp_ref[:, d * CAP : (d + 1) * CAP] = one_hot(block[K : K + 1].astype(I32), PATCHES).astype(BF)
    fill(0)

    all_of(tsend_ref, trecv_ref, t_s, t_r).wait()
    load = []
    for c in range(3):
        line_c = jnp.concatenate([trecv_ref[d, c : c + 1, :] for d in range(N_DOM)], axis=1)
        load.append(wall_ref[...] * line_c)
    by_patch = joined(dot_t(halves(jnp.concatenate(load, axis=0)), ohp_ref[...]))
    spread = []
    for c in range(3):
        line_c = jnp.concatenate([by_patch[c * K + k : c * K + k + 1] for k in range(K)], axis=1)
        spread.append(line_c * maskn_ref[...])
    partial = joined(dot_t(halves(jnp.concatenate(spread, axis=0)), ohn_ref[...]))
    ebuf_ref[...] = partial
    sums = [copy(ebuf_ref, erecv_ref.at[d], e_s.at[0], e_r.at[0], sec_peer(d)) for d in range(1, N_SEC)]
    for c in sums:
        c.start()
    erecv_ref[0] = partial

    for lot in flow:
        for c in lot:
            c.wait()
    extract(lambda w: hhi_ref[w * 128 : w * 128 + 128, :] * keep_hi, PARTS - 1, slice(0, HALO))
    extract(lambda w: hlo_ref[w * 128 : w * 128 + 128, :] * keep_lo, PARTS - 1, slice(HALO, 2 * HALO))
    fill(1)
    all_of(erecv_ref, erecv_ref, e_s, e_r).wait()
    external = erecv_ref[lax.rem(sec, N_SEC)]
    for s in range(1, N_SEC):
        external = external + erecv_ref[lax.rem(sec - s + N_SEC, N_SEC)]

    mass = jnp.concatenate([m_ref[...]] * 3, axis=0)
    for step in range(STEPS):
        if step > 0:
            edges(step)
            around = rims(step)
            for c in around:
                c.start()
            fill(2)
            for c in around:
                c.wait()
            inner = internal(step)
        velocity = v_ref[...] + SHELL_STEP * mass * (external - inner)
        v_ref[...] = velocity
        d_ref[...] = d_ref[...] + SHELL_STEP * velocity

    read = joined(dot(halves(d_ref[...]), ohn_ref[...]))
    nodes = []
    for c in range(3):
        values = jnp.sum(read[c * 8 : c * 8 + 8] * maskn_ref[...], axis=0, keepdims=True)
        nodes += [values[:, k * PATCHES : (k + 1) * PATCHES] for k in range(K)]
    by_row = joined(dot(halves(jnp.concatenate(nodes, axis=0)), ohp_ref[...]))
    rsend_ref[...] = jnp.zeros(rsend_ref.shape, F32)
    for c in range(3):
        total = jnp.sum(by_row[c * K : (c + 1) * K] * wall_ref[...], axis=0, keepdims=True)
        for d in range(N_DOM):
            rsend_ref[d, c : c + 1, :] = total[:, d * CAP : (d + 1) * CAP]
    returns = [
        copy(rsend_ref.at[d], rrecv_ref.at[d], r_s.at[0], r_r.at[0], dom_peer(N_DOM - d)) for d in range(1, N_DOM)
    ]
    for c in returns:
        c.start()
    rrecv_ref[0] = rsend_ref[0]
    for h in range(8):
        for c in range(3):
            shell_ref[c : c + 1, h * 128 : (h + 1) * 128] = d_ref[c * 8 + h : c * 8 + h + 1, :]
    fill(3)
    all_of(rsend_ref, rrecv_ref, r_s, r_r).wait()
    back = joined(dot(halves(rrecv_ref[...].reshape(N_DOM * 8, CAP)), ohs_ref[...]))
    shift = back[0:8] * owned[0:1]
    for d in range(1, N_DOM):
        shift = shift + back[d * 8 : d * 8 + 8] * owned[d : d + 1]
    shift_ref[...] = shift[0:3]


def on_device(
    fluid_state, jac_inv, flux_mats, neighbours, surf_elem, surf_node, normals, rbf_weights, owners,
    patches, patch_nodes, shell_disp, shell_vel, mass_inv, shell_conn, elem_scale, elem_stiff,
):
    own, select, place = constants()
    vmem, hbm = pl.BlockSpec(memory_space=pltpu.VMEM), pl.BlockSpec(memory_space=pl.ANY)
    dma = pltpu.SemaphoreType.DMA
    return pl.pallas_call(
        kernel,
        out_shape=(
            pltpu.VMEM((VARS, NP, E), BF),
            pltpu.VMEM((3, S), F32),
            pltpu.VMEM((3, F), F32),
        ),
        in_specs=[hbm] + [vmem] * 16 + [hbm] * 3,
        out_specs=(vmem, vmem, vmem),
        scratch_shapes=[
            pltpu.VMEM((VARS, NP, E), BF),
            pltpu.VMEM((4, 128, 128), F32),
            pltpu.VMEM((VARS, 6 * 32, 128), BF),
            pltpu.VMEM((6, 128, 128), BF),
            pltpu.VMEM((DEPTH, E), BF),
            pltpu.VMEM((6, PARTS * 128, PART), BF),
            pltpu.VMEM((ROWS, DEPTH), BF),
            pltpu.VMEM((ROWS, HALO), BF),
            pltpu.VMEM((ROWS, HALO), BF),
            pltpu.VMEM((6, (E // HALO + 2) * 32, HALO), BF),
            pltpu.VMEM((2, 6 * 32, HALO), BF),
            pltpu.VMEM((2, 6 * 32, HALO), BF),
            pltpu.VMEM((PATCHES, N_DOM * CAP), BF),
            pltpu.VMEM((128, K * PATCHES), BF),
            pltpu.VMEM((8, K * PATCHES), F32),
            pltpu.VMEM((128, 4 * SE), BF),
            pltpu.VMEM((8, 4 * SE), F32),
            pltpu.VMEM((1, 4 * SE), F32),
            pltpu.VMEM((CAP, F), BF),
            pltpu.VMEM((N_DOM, 32, CAP), BF),
            pltpu.VMEM((N_DOM, 32, CAP), BF),
            pltpu.VMEM((K, N_DOM * CAP), F32),
            pltpu.VMEM((N_DOM, 8, CAP), F32),
            pltpu.VMEM((N_DOM, 8, CAP), F32),
            pltpu.VMEM((N_DOM, 8, CAP), F32),
            pltpu.VMEM((N_DOM, 8, CAP), F32),
            pltpu.VMEM((24, 128), F32),
            pltpu.VMEM((N_SEC, 24, 128), F32),
            pltpu.VMEM((STEPS, 2, 8, 128), F32),
            pltpu.VMEM((STEPS, 2, 8, 128), F32),
            pltpu.VMEM((24, 128), F32),
            pltpu.VMEM((24, 128), F32),
            pltpu.VMEM((8, 128), F32),
            dma((4,)), dma((2,)), dma((2,)), dma((2, 2)), dma((2, 2)),
            dma((1,)), dma((1,)),
            dma((1,)), dma((1,)),
            dma((1,)), dma((1,)),
            dma((1,)), dma((1,)),
            dma((STEPS, 2)), dma((STEPS, 2)),
        ],
        compiler_params=pltpu.CompilerParams(
            collective_id=0, has_side_effects=True, vmem_limit_bytes=56 * 1024 * 1024
        ),
    )(
        fluid_state, jac_inv.reshape(1, E), jnp.transpose(flux_mats, (1, 0, 2)), neighbours, surf_elem.reshape(1, F),
        surf_node.reshape(1, F), normals, rbf_weights, owners.reshape(1, F), patches.reshape(1, F),
        patch_nodes, shell_disp, shell_vel, mass_inv.reshape(1, S), shell_conn,
        elem_scale.reshape(1, SE), elem_stiff, jnp.asarray(own), jnp.asarray(select), jnp.asarray(place),
    )


def solution(mesh):
    flow, shell = ("sec", "dom"), "dom"
    return jax.shard_map(
        on_device,
        mesh=mesh,
        in_specs=(
            P(None, None, flow),
            P(flow),
            P(),
            P(None, flow),
            P(flow),
            P(flow),
            P(None, flow),
            P(None, flow),
            P(flow, None),
            P(flow),
            P(None, shell),
            P(None, shell),
            P(None, shell),
            P(shell),
            P(None, shell),
            P(shell),
            P(),
        ),
        out_specs=(P(None, None, flow), P(None, shell), P(None, flow)),
        check_vma=False,
    )
```
